32 devices in a mesh: grp: 2 (over x), row: 16 (over z, y, core).
Axes of the slice: x: 2, y: 2, z: 4, core: 2. Of those that a mesh axis runs over, the one named last changes fastest.
Arguments:
- inputs: bfloat16 [8192, 8192], P(('grp', 'row')), parts along dimension 0, may hold values from -6 to 6
- out_grads: bfloat16 [8192, 8192], P(('grp', 'row')), parts along dimension 0, may hold values from -6 to 6
- proj_in: bfloat16 [8192, 64], replicated, may hold values from -0.0625 to 0.0625
- proj_out: bfloat16 [8192, 64], replicated, may hold values from -0.0625 to 0.0625
- example_ids: int32 [8192], P(('grp', 'row')), parts along dimension 0, may hold values from 0 to 7, as said below
Outputs:
- gram: float32 [256, 128], P(('grp', 'row')), parts along dimension 0
The draws below stay inside these ranges and needn't reach their ends.
There are 2 independent parts, one for each index of `grp`. The reference program is written for one: setup_inputs(seed, part) draws one part's arguments, and reference() takes and returns one part's arrays. A program takes and returns all parts, laid end to end along the dimension named above; an argument that names none is the same for every part. Nothing has to cross between parts.
Inputs may be any that keep to these rules, and one draw needn't show every extreme that they name: `example_ids`: within each aligned block of 256 tokens every value 0 to 7 appears exactly 32 times, in an order drawn from the seed.
All inputs are finite; a program needn't handle non-finite values.
Results may differ from the reference program's by a relative error of at most 0.0025.
Values may be sent and summed in bfloat16 or wider, within the bound.
A program may use at most 64 MiB of HBM per device.

```python
import math
import jax
import jax.numpy as jnp

D = 8192
RANK = 64
TPE = 32
EX_DEV = 8
TOK_DEV = 256
EXAMPLES = 128
TOKENS = 4096


def draw_example_ids(key, part):
    blocks = TOKENS // TOK_DEV
    pattern = jnp.arange(TOK_DEV, dtype=jnp.int32) // TPE
    splits = jax.random.split(jax.random.fold_in(key, 11), blocks)
    shuffled = jax.vmap(lambda subkey: jax.random.permutation(subkey, pattern))(splits)
    return shuffled.reshape(TOKENS).astype(jnp.int32)


def shard_levels(stream_key, shape, pieces, low, top_value):
    level, own = 1.0, jax.random.fold_in(stream_key, 6)
    for dim, parts in pieces:
        heights = jnp.exp(jax.random.uniform(jax.random.fold_in(own, dim), (parts,), jnp.float32, low / len(pieces), top_value / len(pieces)))
        level = level * jnp.repeat(heights, shape[dim] // parts).reshape([-1 if axis == dim else 1 for axis in range(len(shape))])
    return level


def bell_draw(key, dims, spread, bound, cuts=(), kind=jnp.bfloat16):
    drawn = spread * jax.random.normal(key, dims, jnp.float32)
    if cuts:
        drawn = drawn * shard_levels(key, dims, cuts, -0.22, 0.18)
    return jnp.clip(drawn, -bound, bound).astype(kind)


def setup_inputs(seed: int = 0, part: int = 0) -> dict:
    arg_keys = jax.random.split(jax.random.key(seed), 6)
    own_keys = jax.random.split(jax.random.fold_in(arg_keys[5], part), 6)
    inputs = bell_draw(own_keys[0], (TOKENS, D), 1.0, 6.0, ((0, 16),))
    out_grads = bell_draw(own_keys[1], (TOKENS, D), 1.0, 6.0, ((0, 16),))
    proj_in = bell_draw(arg_keys[2], (D, RANK), D ** -0.5, 0.0625)
    proj_out = bell_draw(arg_keys[3], (D, RANK), D ** -0.5, 0.0625)
    example_ids = draw_example_ids(jax.random.fold_in(jax.random.fold_in(arg_keys[5], part), 71), part)
    return dict(inputs=inputs, out_grads=out_grads, proj_in=proj_in, proj_out=proj_out, example_ids=example_ids)


def reference(inputs, out_grads, proj_in, proj_out, example_ids):
    xproj = jnp.dot(inputs, proj_in, preferred_element_type=jnp.float32).astype(jnp.bfloat16)
    gproj = jnp.dot(out_grads, proj_out, preferred_element_type=jnp.float32).astype(jnp.bfloat16)
    blocks = TOKENS // TOK_DEV
    block_ids = example_ids.reshape(blocks, TOK_DEV)
    onehot = (block_ids[:, None, :] == jnp.arange(EX_DEV, dtype=jnp.int32)[None, :, None]).astype(jnp.float32)
    grad_blocks = gproj.astype(jnp.float32).reshape(blocks, TOK_DEV, RANK)
    input_blocks = xproj.astype(jnp.float32).reshape(blocks, TOK_DEV, RANK)
    weighted = onehot[:, :, :, None] * grad_blocks[:, None, :, :]
    outer = jnp.einsum('betp,btq->bepq', weighted, input_blocks)
    scale_factor = 1.0 / math.sqrt(TPE)
    features = (outer.reshape(EXAMPLES, RANK * RANK) * scale_factor).astype(jnp.bfloat16)
    gram = jnp.dot(features, features.T, preferred_element_type=jnp.float32) / RANK
    return gram
```

```python
import functools
import math

import jax
import jax.numpy as jnp
from jax import lax
from jax.experimental import pallas as pl
from jax.experimental.pallas import tpu as pltpu
from jax.sharding import PartitionSpec as P

RANK = 64
TPE = 32
EX_DEV = 8
LANES = 128
SLICES = 16
CHUNK = 1024
MESH = pl.DeviceIdType.MESH
NT = (((1,), (1,)), ((), ()))


def dot_nt(a, b):
    return lax.dot_general(a, b, NT, preferred_element_type=jnp.float32)


def kernel(
    n,
    x_hbm,
    g_hbm,
    pi_hbm,
    po_hbm,
    ids_hbm,
    out_ref,
    x_buf,
    g_buf,
    pi_buf,
    po_buf,
    ids_ref,
    feat,
    recv,
    gram,
    parts,
    load_sem,
    ids_sem,
    send_a,
    recv_a,
    send_b,
    recv_b,
):
    me = lax.axis_index("row")
    quarter, mine = me // SLICES, me % SLICES
    chunks = x_buf.shape[1] // CHUNK

    loads = []
    for c in range(chunks):
        cols = pl.ds(c * CHUNK, CHUNK)
        pairs = ((pi_hbm, pi_buf), (x_hbm, x_buf), (po_hbm, po_buf), (g_hbm, g_buf))
        loads.append(
            [
                pltpu.make_async_copy(src.at[:, cols], dst.at[:, cols], load_sem.at[c, i])
                for i, (src, dst) in enumerate(pairs)
            ]
        )
        for copy in loads[-1]:
            copy.start()

    ids_copy = pltpu.make_async_copy(ids_hbm, ids_ref, ids_sem)
    ids_copy.start()

    barrier = pltpu.get_barrier_semaphore()
    for d in range(1, n):
        pl.semaphore_signal(
            barrier, inc=1, device_id={"row": lax.rem(me + d, n)}, device_id_type=MESH
        )

    tokens = x_buf.shape[0]
    x = jnp.zeros((tokens, 2 * RANK), jnp.float32)
    g = jnp.zeros((tokens, 2 * RANK), jnp.float32)
    for c in range(chunks):
        cols = pl.ds(c * CHUNK, CHUNK)
        loads[c][0].wait()
        loads[c][1].wait()
        pi = pi_buf[:, cols]
        x += dot_nt(x_buf[:, cols], jnp.concatenate([pi, pi], axis=0))
        loads[c][2].wait()
        loads[c][3].wait()
        po = po_buf[:, cols]
        g += dot_nt(g_buf[:, cols], jnp.concatenate([po, po], axis=0))

    x = x.astype(jnp.bfloat16)
    g = g.astype(jnp.bfloat16).astype(jnp.float32).T[:RANK]
    ids_copy.wait()
    ids = ids_ref[...].reshape(1, tokens)
    onehot = (ids == lax.broadcasted_iota(jnp.int32, (EX_DEV, tokens), 0)).astype(jnp.float32)
    weighted = (g[:, None, :] * onehot[None, :, :]).reshape(RANK * EX_DEV, tokens)
    outer = jnp.dot(weighted.astype(jnp.bfloat16), x, preferred_element_type=jnp.float32)
    half = RANK * EX_DEV // 2
    low = lax.broadcasted_iota(jnp.int32, (half, LANES), 1) < RANK
    packed = jnp.where(low, outer[:half], outer[half:]) * (1.0 / math.sqrt(TPE))
    feat[...] = packed.astype(jnp.bfloat16).reshape(feat.shape)

    pl.semaphore_wait(barrier, n - 1)
    for d in range(1, n):
        target = lax.rem(me + d, n)
        pltpu.make_async_remote_copy(
            src_ref=feat.at[lax.rem(target, SLICES)],
            dst_ref=recv.at[me],
            send_sem=send_a,
            recv_sem=recv_a,
            device_id={"row": target},
            device_id_type=MESH,
        ).start()
    recv[me] = feat[mine]
    rest = recv.at[pl.ds(0, n - 1)]
    pltpu.make_async_copy(rest, rest, recv_a).wait()

    def rows(block):
        block = block.astype(jnp.float32).reshape(-1, 2, EX_DEV, LANES)
        sides = [block[:, i].reshape(-1, LANES) for i in range(2)]
        return jnp.concatenate(sides, axis=1).astype(jnp.bfloat16)

    every = rows(recv[...])
    own = every if n == SLICES else rows(recv[pl.ds(quarter * SLICES, SLICES)])
    gram[...] = dot_nt(own, every).reshape(gram.shape)

    for d in range(1, SLICES):
        to = lax.rem(mine + d, SLICES)
        pltpu.make_async_remote_copy(
            src_ref=gram.at[to],
            dst_ref=parts.at[mine],
            send_sem=send_b,
            recv_sem=recv_b,
            device_id={"row": quarter * SLICES + to},
            device_id_type=MESH,
        ).start()
    parts[mine] = gram[mine]
    rest_b = parts.at[pl.ds(0, SLICES - 1)]
    pltpu.make_async_copy(rest_b, rest_b, recv_b).wait()
    out_ref[...] = jnp.sum(parts[...], axis=0) * (1.0 / RANK)
    pltpu.make_async_copy(rest, rest, send_a).wait()
    pltpu.make_async_copy(rest_b, rest_b, send_b).wait()


def shards(n, inputs, out_grads, proj_in, proj_out, example_ids):
    tokens, width = inputs.shape
    examples = EX_DEV * n
    hbm = pl.BlockSpec(memory_space=pl.ANY)
    vmem = pl.BlockSpec(memory_space=pltpu.VMEM)
    flops = 4 * tokens * width * RANK
    return pl.pallas_call(
        functools.partial(kernel, n),
        out_shape=jax.ShapeDtypeStruct((EX_DEV, examples), jnp.float32),
        in_specs=[hbm] * 5,
        out_specs=vmem,
        scratch_shapes=[
            pltpu.VMEM((tokens, width), jnp.bfloat16),
            pltpu.VMEM((tokens, width), jnp.bfloat16),
            pltpu.VMEM((RANK, width), jnp.bfloat16),
            pltpu.VMEM((RANK, width), jnp.bfloat16),
            pltpu.VMEM((tokens,), jnp.int32),
            pltpu.VMEM((SLICES, 2 * EX_DEV, LANES), jnp.bfloat16),
            pltpu.VMEM((n, 2 * EX_DEV, LANES), jnp.bfloat16),
            pltpu.VMEM((SLICES, EX_DEV, examples), jnp.float32),
            pltpu.VMEM((SLICES, EX_DEV, examples), jnp.float32),
            pltpu.SemaphoreType.DMA((width // CHUNK, 4)),
            pltpu.SemaphoreType.DMA,
            pltpu.SemaphoreType.DMA,
            pltpu.SemaphoreType.DMA,
            pltpu.SemaphoreType.DMA,
            pltpu.SemaphoreType.DMA,
        ],
        compiler_params=pltpu.CompilerParams(
            collective_id=0, has_side_effects=True, vmem_limit_bytes=63 * 1024 * 1024
        ),
        cost_estimate=pl.CostEstimate(
            flops=flops, bytes_accessed=4 * (tokens + RANK) * width, transcendentals=0
        ),
    )(inputs, out_grads, proj_in.T, proj_out.T, example_ids)


def solution(mesh):
    in_specs = (P(("grp", "row"), None), P(("grp", "row"), None), P(), P(), P(("grp", "row")))
    out_specs = P(("grp", "row"), None)
    body = functools.partial(shards, mesh.shape["row"])
    return jax.shard_map(body, mesh=mesh, in_specs=in_specs, out_specs=out_specs, check_vma=False)
```

```python
import functools
import math

import jax
import jax.numpy as jnp
from jax import lax
from jax.experimental import pallas as pl
from jax.experimental.pallas import tpu as pltpu
from jax.sharding import PartitionSpec as P

RANK = 64
TPE = 32
EX_DEV = 8
LANES = 128
SLICES = 16
CHUNK = 1024
MESH = pl.DeviceIdType.MESH
NT = (((1,), (1,)), ((), ()))


def dot_nt(a, b):
    return lax.dot_general(a, b, NT, preferred_element_type=jnp.float32)


def kernel(
    n,
    x_hbm,
    g_hbm,
    pi_hbm,
    po_hbm,
    ids_hbm,
    out_ref,
    x_buf,
    g_buf,
    pi_buf,
    po_buf,
    ids_ref,
    x_sum,
    g_sum,
    feat,
    recv,
    gram,
    parts,
    load_sem,
    ids_sem,
    send_a,
    recv_a,
    send_b,
    recv_b,
):
    me = lax.axis_index("row")
    quarter, mine = me // SLICES, me % SLICES
    chunks = x_buf.shape[1] // CHUNK

    pairs = ((pi_hbm, pi_buf), (x_hbm, x_buf), (po_hbm, po_buf), (g_hbm, g_buf))

    def loads(c):
        cols = pl.ds(pl.multiple_of(c * CHUNK, CHUNK), CHUNK)
        return cols, [
            pltpu.make_async_copy(src.at[:, cols], dst.at[:, cols], load_sem.at[c, i])
            for i, (src, dst) in enumerate(pairs)
        ]

    @pl.loop(0, chunks)
    def _(c):
        for copy in loads(c)[1]:
            copy.start()

    ids_copy = pltpu.make_async_copy(ids_hbm, ids_ref, ids_sem)
    ids_copy.start()

    barrier = pltpu.get_barrier_semaphore()
    for d in range(1, n):
        pl.semaphore_signal(
            barrier, inc=1, device_id={"row": lax.rem(me + d, n)}, device_id_type=MESH
        )

    tokens = x_buf.shape[0]
    x_sum[...] = jnp.zeros_like(x_sum)
    g_sum[...] = jnp.zeros_like(g_sum)

    @pl.loop(0, chunks)
    def _(c):
        cols, copies = loads(c)
        copies[0].wait()
        copies[1].wait()
        pi = pi_buf[:, cols]
        x_sum[...] += dot_nt(x_buf[:, cols], jnp.concatenate([pi, pi], axis=0))
        copies[2].wait()
        copies[3].wait()
        po = po_buf[:, cols]
        g_sum[...] += dot_nt(g_buf[:, cols], jnp.concatenate([po, po], axis=0))

    x = x_sum[...].astype(jnp.bfloat16)
    g = g_sum[...].astype(jnp.bfloat16).astype(jnp.float32).T[:RANK]
    ids_copy.wait()
    ids = ids_ref[...].reshape(1, tokens)
    onehot = (ids == lax.broadcasted_iota(jnp.int32, (EX_DEV, tokens), 0)).astype(jnp.float32)
    weighted = (g[:, None, :] * onehot[None, :, :]).reshape(RANK * EX_DEV, tokens)
    outer = jnp.dot(weighted.astype(jnp.bfloat16), x, preferred_element_type=jnp.float32)
    half = RANK * EX_DEV // 2
    low = lax.broadcasted_iota(jnp.int32, (half, LANES), 1) < RANK
    packed = jnp.where(low, outer[:half], outer[half:]) * (1.0 / math.sqrt(TPE))
    feat[...] = packed.astype(jnp.bfloat16).reshape(feat.shape)

    pl.semaphore_wait(barrier, n - 1)
    for d in range(1, n):
        target = lax.rem(me + d, n)
        pltpu.make_async_remote_copy(
            src_ref=feat.at[lax.rem(target, SLICES)],
            dst_ref=recv.at[me],
            send_sem=send_a,
            recv_sem=recv_a,
            device_id={"row": target},
            device_id_type=MESH,
        ).start()
    recv[me] = feat[mine]
    rest = recv.at[pl.ds(0, n - 1)]
    pltpu.make_async_copy(rest, rest, recv_a).wait()

    def rows(block):
        block = block.astype(jnp.float32).reshape(-1, 2, EX_DEV, LANES)
        sides = [block[:, i].reshape(-1, LANES) for i in range(2)]
        return jnp.concatenate(sides, axis=1).astype(jnp.bfloat16)

    every = rows(recv[...])
    own = every if n == SLICES else rows(recv[pl.ds(quarter * SLICES, SLICES)])
    gram[...] = dot_nt(own, every).reshape(gram.shape)

    for d in range(1, SLICES):
        to = lax.rem(mine + d, SLICES)
        pltpu.make_async_remote_copy(
            src_ref=gram.at[to],
            dst_ref=parts.at[mine],
            send_sem=send_b,
            recv_sem=recv_b,
            device_id={"row": quarter * SLICES + to},
            device_id_type=MESH,
        ).start()
    parts[mine] = gram[mine]
    rest_b = parts.at[pl.ds(0, SLICES - 1)]
    pltpu.make_async_copy(rest_b, rest_b, recv_b).wait()
    out_ref[...] = jnp.sum(parts[...], axis=0) * (1.0 / RANK)
    pltpu.make_async_copy(rest, rest, send_a).wait()
    pltpu.make_async_copy(rest_b, rest_b, send_b).wait()


def shards(n, inputs, out_grads, proj_in, proj_out, example_ids):
    tokens, width = inputs.shape
    examples = EX_DEV * n
    hbm = pl.BlockSpec(memory_space=pl.ANY)
    vmem = pl.BlockSpec(memory_space=pltpu.VMEM)
    flops = 4 * tokens * width * RANK
    return pl.pallas_call(
        functools.partial(kernel, n),
        out_shape=jax.ShapeDtypeStruct((EX_DEV, examples), jnp.float32),
        in_specs=[hbm] * 5,
        out_specs=vmem,
        scratch_shapes=[
            pltpu.VMEM((tokens, width), jnp.bfloat16),
            pltpu.VMEM((tokens, width), jnp.bfloat16),
            pltpu.VMEM((RANK, width), jnp.bfloat16),
            pltpu.VMEM((RANK, width), jnp.bfloat16),
            pltpu.VMEM((tokens,), jnp.int32),
            pltpu.VMEM((tokens, 2 * RANK), jnp.float32),
            pltpu.VMEM((tokens, 2 * RANK), jnp.float32),
            pltpu.VMEM((SLICES, 2 * EX_DEV, LANES), jnp.bfloat16),
            pltpu.VMEM((n, 2 * EX_DEV, LANES), jnp.bfloat16),
            pltpu.VMEM((SLICES, EX_DEV, examples), jnp.float32),
            pltpu.VMEM((SLICES, EX_DEV, examples), jnp.float32),
            pltpu.SemaphoreType.DMA((width // CHUNK, 4)),
            pltpu.SemaphoreType.DMA,
            pltpu.SemaphoreType.DMA,
            pltpu.SemaphoreType.DMA,
            pltpu.SemaphoreType.DMA,
            pltpu.SemaphoreType.DMA,
        ],
        compiler_params=pltpu.CompilerParams(
            collective_id=0, has_side_effects=True, vmem_limit_bytes=63 * 1024 * 1024
        ),
        cost_estimate=pl.CostEstimate(
            flops=flops, bytes_accessed=4 * (tokens + RANK) * width, transcendentals=0
        ),
    )(inputs, out_grads, proj_in.T, proj_out.T, example_ids)


def solution(mesh):
    in_specs = (P(("grp", "row"), None), P(("grp", "row"), None), P(), P(), P(("grp", "row")))
    out_specs = P(("grp", "row"), None)
    body = functools.partial(shards, mesh.shape["row"])
    return jax.shard_map(body, mesh=mesh, in_specs=in_specs, out_specs=out_specs, check_vma=False)
```

```python
import functools
import math

import jax
import jax.numpy as jnp
from jax import lax
from jax.experimental import pallas as pl
from jax.experimental.pallas import tpu as pltpu
from jax.sharding import PartitionSpec as P

RANK = 64
TPE = 32
EX_DEV = 8
LANES = 128
SLICES = 16
CHUNK = 1024
NEAR = 4
MESH = pl.DeviceIdType.MESH
NT = (((1,), (1,)), ((), ()))


def dot_nt(a, b):
    return lax.dot_general(a, b, NT, preferred_element_type=jnp.float32)


def partner(me, n, i):
    blocks = n // NEAR
    block, place = me // NEAR, me % NEAR
    if i >= n - NEAR:
        return block * NEAR + (place + 1 + i - (n - NEAR)) % NEAR
    step = i // NEAR
    up = blocks - 1 - step
    up = jnp.where(up <= block, up - 1, up)
    down = jnp.where(step >= block, step + 1, step)
    return jnp.where(2 * block < blocks, up, down) * NEAR + (place + i) % NEAR


def kernel(
    n,
    x_hbm,
    g_hbm,
    pi_hbm,
    po_hbm,
    ids_hbm,
    out_ref,
    x_buf,
    g_buf,
    pi_buf,
    po_buf,
    ids_ref,
    x_sum,
    g_sum,
    feat,
    recv,
    gram,
    parts,
    load_sem,
    ids_sem,
    send_a,
    recv_a,
    send_b,
    recv_b,
):
    me = lax.axis_index("row")
    quarter, mine = me // SLICES, me % SLICES
    chunks = x_buf.shape[1] // CHUNK

    barrier = pltpu.get_barrier_semaphore()
    for i in range(n - 1):
        pl.semaphore_signal(
            barrier, inc=1, device_id={"row": partner(me, n, i)}, device_id_type=MESH
        )

    pairs = ((pi_hbm, pi_buf), (x_hbm, x_buf), (po_hbm, po_buf), (g_hbm, g_buf))

    def loads(c):
        cols = pl.ds(pl.multiple_of(c * CHUNK, CHUNK), CHUNK)
        return cols, [
            pltpu.make_async_copy(src.at[:, cols], dst.at[:, cols], load_sem.at[c, i])
            for i, (src, dst) in enumerate(pairs)
        ]

    @pl.loop(0, chunks)
    def _(c):
        for copy in loads(c)[1]:
            copy.start()

    ids_copy = pltpu.make_async_copy(ids_hbm, ids_ref, ids_sem)
    ids_copy.start()

    tokens = x_buf.shape[0]
    x_sum[...] = jnp.zeros_like(x_sum)
    g_sum[...] = jnp.zeros_like(g_sum)

    @pl.loop(0, chunks)
    def _(c):
        cols, copies = loads(c)
        copies[0].wait()
        copies[1].wait()
        x_sum[...] += dot_nt(x_buf[:, cols], pi_buf[:, cols])
        copies[2].wait()
        copies[3].wait()
        g_sum[...] += dot_nt(g_buf[:, cols], po_buf[:, cols])

    x = x_sum[...]
    x = jnp.concatenate([x, x], axis=1).astype(jnp.bfloat16)
    g = g_sum[...].astype(jnp.bfloat16).astype(jnp.float32).T
    ids_copy.wait()
    ids = ids_ref[...].reshape(1, tokens)
    onehot = (ids == lax.broadcasted_iota(jnp.int32, (EX_DEV, tokens), 0)).astype(jnp.float32)
    weighted = (g[:, None, :] * onehot[None, :, :]).reshape(RANK * EX_DEV, tokens)
    outer = jnp.dot(weighted.astype(jnp.bfloat16), x, preferred_element_type=jnp.float32)
    half = RANK * EX_DEV // 2
    low = lax.broadcasted_iota(jnp.int32, (half, LANES), 1) < RANK
    packed = jnp.where(low, outer[:half], outer[half:]) * (1.0 / math.sqrt(TPE))
    feat[...] = packed.astype(jnp.bfloat16).reshape(feat.shape)

    pl.semaphore_wait(barrier, n - 1)
    for i in range(n - 1):
        target = partner(me, n, i)
        pltpu.make_async_remote_copy(
            src_ref=feat.at[lax.rem(target, SLICES)],
            dst_ref=recv.at[me],
            send_sem=send_a,
            recv_sem=recv_a,
            device_id={"row": target},
            device_id_type=MESH,
        ).start()
    recv[me] = feat[mine]
    rest = recv.at[pl.ds(0, n - 1)]
    pltpu.make_async_copy(rest, rest, recv_a).wait()

    def rows(block):
        block = block.astype(jnp.float32).reshape(-1, 2, EX_DEV, LANES)
        sides = [block[:, i].reshape(-1, LANES) for i in range(2)]
        return jnp.concatenate(sides, axis=1).astype(jnp.bfloat16)

    every = rows(recv[...])
    own = every if n == SLICES else rows(recv[pl.ds(quarter * SLICES, SLICES)])
    gram[...] = dot_nt(own, every).reshape(gram.shape)

    for i in range(SLICES - 1):
        to = partner(mine, SLICES, i)
        pltpu.make_async_remote_copy(
            src_ref=gram.at[to],
            dst_ref=parts.at[mine],
            send_sem=send_b,
            recv_sem=recv_b,
            device_id={"row": quarter * SLICES + to},
            device_id_type=MESH,
        ).start()
    parts[mine] = gram[mine]
    rest_b = parts.at[pl.ds(0, SLICES - 1)]
    pltpu.make_async_copy(rest_b, rest_b, recv_b).wait()
    out_ref[...] = jnp.sum(parts[...], axis=0) * (1.0 / RANK)
    pltpu.make_async_copy(rest, rest, send_a).wait()
    pltpu.make_async_copy(rest_b, rest_b, send_b).wait()


def shards(n, inputs, out_grads, proj_in, proj_out, example_ids):
    tokens, width = inputs.shape
    examples = EX_DEV * n
    hbm = pl.BlockSpec(memory_space=pl.ANY)
    vmem = pl.BlockSpec(memory_space=pltpu.VMEM)
    flops = 4 * tokens * width * RANK
    return pl.pallas_call(
        functools.partial(kernel, n),
        out_shape=pltpu.VMEM((EX_DEV, examples), jnp.float32),
        in_specs=[hbm] * 5,
        out_specs=vmem,
        scratch_shapes=[
            pltpu.VMEM((tokens, width), jnp.bfloat16),
            pltpu.VMEM((tokens, width), jnp.bfloat16),
            pltpu.VMEM((RANK, width), jnp.bfloat16),
            pltpu.VMEM((RANK, width), jnp.bfloat16),
            pltpu.VMEM((tokens,), jnp.int32),
            pltpu.VMEM((tokens, RANK), jnp.float32),
            pltpu.VMEM((tokens, RANK), jnp.float32),
            pltpu.VMEM((SLICES, 2 * EX_DEV, LANES), jnp.bfloat16),
            pltpu.VMEM((n, 2 * EX_DEV, LANES), jnp.bfloat16),
            pltpu.VMEM((SLICES, EX_DEV, examples), jnp.float32),
            pltpu.VMEM((SLICES, EX_DEV, examples), jnp.float32),
            pltpu.SemaphoreType.DMA((width // CHUNK, 4)),
            pltpu.SemaphoreType.DMA,
            pltpu.SemaphoreType.DMA,
            pltpu.SemaphoreType.DMA,
            pltpu.SemaphoreType.DMA,
            pltpu.SemaphoreType.DMA,
        ],
        compiler_params=pltpu.CompilerParams(
            collective_id=0, has_side_effects=True, vmem_limit_bytes=63 * 1024 * 1024
        ),
        cost_estimate=pl.CostEstimate(
            flops=flops, bytes_accessed=4 * (tokens + RANK) * width, transcendentals=0
        ),
    )(inputs, out_grads, proj_in.T, proj_out.T, example_ids)


def solution(mesh):
    in_specs = (P(("grp", "row"), None), P(("grp", "row"), None), P(), P(), P(("grp", "row")))
    out_specs = P(("grp", "row"), None)
    body = functools.partial(shards, mesh.shape["row"])
    return jax.shard_map(body, mesh=mesh, in_specs=in_specs, out_specs=out_specs, check_vma=False)
```

```python
import functools
import math

import jax
import jax.numpy as jnp
from jax import lax
from jax.experimental import pallas as pl
from jax.experimental.pallas import tpu as pltpu
from jax.sharding import PartitionSpec as P

RANK = 64
TPE = 32
EX_DEV = 8
LANES = 128
SLICES = 16
CHUNK = 1024
NEAR = 4
MESH = pl.DeviceIdType.MESH
NT = (((1,), (1,)), ((), ()))


def dot_nt(a, b):
    return lax.dot_general(a, b, NT, preferred_element_type=jnp.float32)


def partner(me, n, i):
    blocks = n // NEAR
    block, place = me // NEAR, me % NEAR
    if i >= n - NEAR:
        return block * NEAR + (place + 1 + i - (n - NEAR)) % NEAR
    step = i // NEAR
    up = blocks - 1 - step
    up = jnp.where(up <= block, up - 1, up)
    down = jnp.where(step >= block, step + 1, step)
    return jnp.where(2 * block < blocks, up, down) * NEAR + (place + i) % NEAR


def kernel(
    n,
    x_hbm,
    g_hbm,
    pi_hbm,
    po_hbm,
    ids_hbm,
    out_ref,
    x_buf,
    g_buf,
    pi_buf,
    po_buf,
    ids_ref,
    x_sum,
    g_sum,
    weighted,
    feat,
    recv,
    gram,
    parts,
    load_sem,
    factor_sem,
    ids_sem,
    send_a,
    recv_a,
    send_b,
    recv_b,
):
    me = lax.axis_index("row")
    quarter, mine = me // SLICES, me % SLICES
    chunks = x_buf.shape[1] // CHUNK

    barrier = pltpu.get_barrier_semaphore()
    for i in range(n - 1):
        pl.semaphore_signal(
            barrier, inc=1, device_id={"row": partner(me, n, i)}, device_id_type=MESH
        )

    def load(src, dst, side, c):
        cols = pl.ds(pl.multiple_of(c * CHUNK, CHUNK), CHUNK)
        return cols, pltpu.make_async_copy(src.at[:, cols], dst.at[:, cols], load_sem.at[side, c])

    factors = [
        pltpu.make_async_copy(po_hbm, po_buf, factor_sem.at[0]),
        pltpu.make_async_copy(pi_hbm, pi_buf, factor_sem.at[1]),
    ]
    ids_copy = pltpu.make_async_copy(ids_hbm, ids_ref, ids_sem)
    ids_copy.start()
    streams = ((g_hbm, g_buf, 0), (x_hbm, x_buf, 1))
    for factor, stream in zip(factors, streams):
        factor.start()

        @pl.loop(0, chunks)
        def _(c):
            load(*stream, c)[1].start()

    def project(factor, stream, factor_buf, total):
        total[...] = jnp.zeros_like(total)
        factor.wait()

        @pl.loop(0, chunks)
        def _(c):
            cols, copy = load(*stream, c)
            copy.wait()
            total[...] += dot_nt(stream[1][:, cols], factor_buf[:, cols])

        return total[...]

    tokens = x_buf.shape[0]
    g = project(factors[0], streams[0], po_buf, g_sum)
    g = g.astype(jnp.bfloat16).astype(jnp.float32).T
    ids_copy.wait()
    ids = ids_ref[...].reshape(1, tokens)
    onehot = (ids == lax.broadcasted_iota(jnp.int32, (EX_DEV, tokens), 0)).astype(jnp.float32)
    masked = (g[:, None, :] * onehot[None, :, :]).reshape(RANK * EX_DEV, tokens)
    weighted[...] = masked.astype(jnp.bfloat16)

    x = project(factors[1], streams[1], pi_buf, x_sum)
    x = jnp.concatenate([x, x], axis=1).astype(jnp.bfloat16)
    outer = jnp.dot(weighted[...], x, preferred_element_type=jnp.float32)
    half = RANK * EX_DEV // 2
    low = lax.broadcasted_iota(jnp.int32, (half, LANES), 1) < RANK
    packed = jnp.where(low, outer[:half], outer[half:]) * (1.0 / math.sqrt(TPE))
    feat[...] = packed.astype(jnp.bfloat16).reshape(feat.shape)

    pl.semaphore_wait(barrier, n - 1)
    for i in range(n - 1):
        target = partner(me, n, i)
        pltpu.make_async_remote_copy(
            src_ref=feat.at[lax.rem(target, SLICES)],
            dst_ref=recv.at[me],
            send_sem=send_a,
            recv_sem=recv_a,
            device_id={"row": target},
            device_id_type=MESH,
        ).start()
    recv[me] = feat[mine]
    rest = recv.at[pl.ds(0, n - 1)]
    pltpu.make_async_copy(rest, rest, recv_a).wait()

    def rows(block):
        block = block.astype(jnp.float32).reshape(-1, 2, EX_DEV, LANES)
        sides = [block[:, i].reshape(-1, LANES) for i in range(2)]
        return jnp.concatenate(sides, axis=1).astype(jnp.bfloat16)

    every = rows(recv[...])
    own = every if n == SLICES else rows(recv[pl.ds(quarter * SLICES, SLICES)])
    gram[...] = dot_nt(own, every).reshape(gram.shape)

    for i in range(SLICES - 1):
        to = partner(mine, SLICES, i)
        pltpu.make_async_remote_copy(
            src_ref=gram.at[to],
            dst_ref=parts.at[mine],
            send_sem=send_b,
            recv_sem=recv_b,
            device_id={"row": quarter * SLICES + to},
            device_id_type=MESH,
        ).start()
    parts[mine] = gram[mine]
    rest_b = parts.at[pl.ds(0, SLICES - 1)]
    pltpu.make_async_copy(rest_b, rest_b, recv_b).wait()
    out_ref[...] = jnp.sum(parts[...], axis=0) * (1.0 / RANK)
    pltpu.make_async_copy(rest, rest, send_a).wait()
    pltpu.make_async_copy(rest_b, rest_b, send_b).wait()


def shards(n, inputs, out_grads, proj_in, proj_out, example_ids):
    tokens, width = inputs.shape
    examples = EX_DEV * n
    hbm = pl.BlockSpec(memory_space=pl.ANY)
    vmem = pl.BlockSpec(memory_space=pltpu.VMEM)
    flops = 4 * tokens * width * RANK
    return pl.pallas_call(
        functools.partial(kernel, n),
        out_shape=pltpu.VMEM((EX_DEV, examples), jnp.float32),
        in_specs=[hbm] * 5,
        out_specs=vmem,
        scratch_shapes=[
            pltpu.VMEM((tokens, width), jnp.bfloat16),
            pltpu.VMEM((tokens, width), jnp.bfloat16),
            pltpu.VMEM((RANK, width), jnp.bfloat16),
            pltpu.VMEM((RANK, width), jnp.bfloat16),
            pltpu.VMEM((tokens,), jnp.int32),
            pltpu.VMEM((tokens, RANK), jnp.float32),
            pltpu.VMEM((tokens, RANK), jnp.float32),
            pltpu.VMEM((RANK * EX_DEV, tokens), jnp.bfloat16),
            pltpu.VMEM((SLICES, 2 * EX_DEV, LANES), jnp.bfloat16),
            pltpu.VMEM((n, 2 * EX_DEV, LANES), jnp.bfloat16),
            pltpu.VMEM((SLICES, EX_DEV, examples), jnp.float32),
            pltpu.VMEM((SLICES, EX_DEV, examples), jnp.float32),
            pltpu.SemaphoreType.DMA((2, width // CHUNK)),
            pltpu.SemaphoreType.DMA((2,)),
            pltpu.SemaphoreType.DMA,
            pltpu.SemaphoreType.DMA,
            pltpu.SemaphoreType.DMA,
            pltpu.SemaphoreType.DMA,
            pltpu.SemaphoreType.DMA,
        ],
        compiler_params=pltpu.CompilerParams(
            collective_id=0, has_side_effects=True, vmem_limit_bytes=63 * 1024 * 1024
        ),
        cost_estimate=pl.CostEstimate(
            flops=flops, bytes_accessed=4 * (tokens + RANK) * width, transcendentals=0
        ),
    )(inputs, out_grads, proj_in.T, proj_out.T, example_ids)


def solution(mesh):
    in_specs = (P(("grp", "row"), None), P(("grp", "row"), None), P(), P(), P(("grp", "row")))
    out_specs = P(("grp", "row"), None)
    body = functools.partial(shards, mesh.shape["row"])
    return jax.shard_map(body, mesh=mesh, in_specs=in_specs, out_specs=out_specs, check_vma=False)
```

```python
import functools
import math

import jax
import jax.numpy as jnp
from jax import lax
from jax.experimental import pallas as pl
from jax.experimental.pallas import tpu as pltpu
from jax.sharding import PartitionSpec as P

RANK = 64
TPE = 32
EX_DEV = 8
LANES = 128
SLICES = 16
CHUNK = 1024
NEAR = 4
MESH = pl.DeviceIdType.MESH
NT = (((1,), (1,)), ((), ()))


def dot_nt(a, b):
    return lax.dot_general(a, b, NT, preferred_element_type=jnp.float32)


def partner(me, n, i):
    blocks = n // NEAR
    block, place = me // NEAR, me % NEAR
    if i >= n - NEAR:
        return block * NEAR + (place + 1 + i - (n - NEAR)) % NEAR
    step = i // NEAR
    up = blocks - 1 - step
    up = jnp.where(up <= block, up - 1, up)
    down = jnp.where(step >= block, step + 1, step)
    return jnp.where(2 * block < blocks, up, down) * NEAR + (place + i) % NEAR


def kernel(
    n,
    x_hbm,
    g_hbm,
    pi_hbm,
    po_hbm,
    ids_hbm,
    out_ref,
    x_buf,
    g_buf,
    pi_buf,
    po_buf,
    ids_ref,
    x_sum,
    g_sum,
    weighted,
    feat,
    recv,
    gram,
    parts,
    load_sem,
    factor_sem,
    ids_sem,
    send_a,
    recv_a,
    send_b,
    recv_b,
):
    me = lax.axis_index("row")
    quarter, mine = me // SLICES, me % SLICES
    chunks = x_buf.shape[1] // CHUNK

    barrier = pltpu.get_barrier_semaphore()
    for i in range(n - 1):
        pl.semaphore_signal(
            barrier, inc=1, device_id={"row": partner(me, n, i)}, device_id_type=MESH
        )

    def load(src, dst, side, c):
        cols = pl.ds(pl.multiple_of(c * CHUNK, CHUNK), CHUNK)
        return cols, pltpu.make_async_copy(src.at[:, cols], dst.at[:, cols], load_sem.at[side, c])

    factors = [
        pltpu.make_async_copy(po_hbm, po_buf, factor_sem.at[0]),
        pltpu.make_async_copy(pi_hbm, pi_buf, factor_sem.at[1]),
    ]
    ids_copy = pltpu.make_async_copy(ids_hbm, ids_ref, ids_sem)
    ids_copy.start()
    streams = ((g_hbm, g_buf, 0), (x_hbm, x_buf, 1))
    for factor, stream in zip(factors, streams):
        factor.start()

        @pl.loop(0, chunks)
        def _(c):
            load(*stream, c)[1].start()

    def project(factor, stream, factor_buf, total):
        total[...] = jnp.zeros_like(total)
        factor.wait()

        @pl.loop(0, chunks)
        def _(c):
            cols, copy = load(*stream, c)
            copy.wait()
            total[...] += dot_nt(factor_buf[:, cols], stream[1][:, cols])

        return total[...]

    tokens = x_buf.shape[0]
    g = project(factors[0], streams[0], po_buf, g_sum)
    g = g.astype(jnp.bfloat16).astype(jnp.float32)
    ids_copy.wait()
    ids = ids_ref[...].reshape(1, tokens)
    onehot = (ids == lax.broadcasted_iota(jnp.int32, (EX_DEV, tokens), 0)).astype(jnp.float32)
    masked = (g[:, None, :] * onehot[None, :, :]).reshape(RANK * EX_DEV, tokens)
    weighted[...] = masked.astype(jnp.bfloat16)

    x = project(factors[1], streams[1], pi_buf, x_sum)
    outer = dot_nt(weighted[...], jnp.concatenate([x, x], axis=0).astype(jnp.bfloat16))
    half = RANK * EX_DEV // 2
    low = lax.broadcasted_iota(jnp.int32, (half, LANES), 1) < RANK
    packed = jnp.where(low, outer[:half], outer[half:]) * (1.0 / math.sqrt(TPE))
    feat[...] = packed.astype(jnp.bfloat16).reshape(feat.shape)

    pl.semaphore_wait(barrier, n - 1)
    for i in range(n - 1):
        target = partner(me, n, i)
        pltpu.make_async_remote_copy(
            src_ref=feat.at[lax.rem(target, SLICES)],
            dst_ref=recv.at[me],
            send_sem=send_a,
            recv_sem=recv_a,
            device_id={"row": target},
            device_id_type=MESH,
        ).start()
    recv[me] = feat[mine]
    rest = recv.at[pl.ds(0, n - 1)]
    pltpu.make_async_copy(rest, rest, recv_a).wait()

    def rows(block):
        block = block.astype(jnp.float32).reshape(-1, 2, EX_DEV, LANES)
        sides = [block[:, i].reshape(-1, LANES) for i in range(2)]
        return jnp.concatenate(sides, axis=1).astype(jnp.bfloat16)

    every = rows(recv[...])
    own = every if n == SLICES else rows(recv[pl.ds(quarter * SLICES, SLICES)])
    gram[...] = dot_nt(own, every).reshape(gram.shape)

    for i in range(SLICES - 1):
        to = partner(mine, SLICES, i)
        pltpu.make_async_remote_copy(
            src_ref=gram.at[to],
            dst_ref=parts.at[mine],
            send_sem=send_b,
            recv_sem=recv_b,
            device_id={"row": quarter * SLICES + to},
            device_id_type=MESH,
        ).start()
    parts[mine] = gram[mine]
    rest_b = parts.at[pl.ds(0, SLICES - 1)]
    pltpu.make_async_copy(rest_b, rest_b, recv_b).wait()
    out_ref[...] = jnp.sum(parts[...], axis=0) * (1.0 / RANK)
    pltpu.make_async_copy(rest, rest, send_a).wait()
    pltpu.make_async_copy(rest_b, rest_b, send_b).wait()


def shards(n, inputs, out_grads, proj_in, proj_out, example_ids):
    tokens, width = inputs.shape
    examples = EX_DEV * n
    hbm = pl.BlockSpec(memory_space=pl.ANY)
    vmem = pl.BlockSpec(memory_space=pltpu.VMEM)
    flops = 4 * tokens * width * RANK
    return pl.pallas_call(
        functools.partial(kernel, n),
        out_shape=pltpu.VMEM((EX_DEV, examples), jnp.float32),
        in_specs=[hbm] * 5,
        out_specs=vmem,
        scratch_shapes=[
            pltpu.VMEM((tokens, width), jnp.bfloat16),
            pltpu.VMEM((tokens, width), jnp.bfloat16),
            pltpu.VMEM((RANK, width), jnp.bfloat16),
            pltpu.VMEM((RANK, width), jnp.bfloat16),
            pltpu.VMEM((tokens,), jnp.int32),
            pltpu.VMEM((RANK, tokens), jnp.float32),
            pltpu.VMEM((RANK, tokens), jnp.float32),
            pltpu.VMEM((RANK * EX_DEV, tokens), jnp.bfloat16),
            pltpu.VMEM((SLICES, 2 * EX_DEV, LANES), jnp.bfloat16),
            pltpu.VMEM((n, 2 * EX_DEV, LANES), jnp.bfloat16),
            pltpu.VMEM((SLICES, EX_DEV, examples), jnp.float32),
            pltpu.VMEM((SLICES, EX_DEV, examples), jnp.float32),
            pltpu.SemaphoreType.DMA((2, width // CHUNK)),
            pltpu.SemaphoreType.DMA((2,)),
            pltpu.SemaphoreType.DMA,
            pltpu.SemaphoreType.DMA,
            pltpu.SemaphoreType.DMA,
            pltpu.SemaphoreType.DMA,
            pltpu.SemaphoreType.DMA,
        ],
        compiler_params=pltpu.CompilerParams(
            collective_id=0, has_side_effects=True, vmem_limit_bytes=63 * 1024 * 1024
        ),
        cost_estimate=pl.CostEstimate(
            flops=flops, bytes_accessed=4 * (tokens + RANK) * width, transcendentals=0
        ),
    )(inputs, out_grads, proj_in.T, proj_out.T, example_ids)


def solution(mesh):
    in_specs = (P(("grp", "row"), None), P(("grp", "row"), None), P(), P(), P(("grp", "row")))
    out_specs = P(("grp", "row"), None)
    body = functools.partial(shards, mesh.shape["row"])
    return jax.shard_map(body, mesh=mesh, in_specs=in_specs, out_specs=out_specs, check_vma=False)
```

```python
import functools
import math

import jax
import jax.numpy as jnp
from jax import lax
from jax.experimental import pallas as pl
from jax.experimental.pallas import tpu as pltpu
from jax.sharding import PartitionSpec as P

RANK = 64
TPE = 32
EX_DEV = 8
LANES = 128
SLICES = 16
CHUNK = 1024
NEAR = 4
MESH = pl.DeviceIdType.MESH
NT = (((1,), (1,)), ((), ()))


def dot_nt(a, b):
    return lax.dot_general(a, b, NT, preferred_element_type=jnp.float32)


def partner(me, n, i):
    blocks = n // NEAR
    block, place = me // NEAR, me % NEAR
    if i >= n - NEAR:
        return block * NEAR + (place + 1 + i - (n - NEAR)) % NEAR
    step = i // NEAR
    up = blocks - 1 - step
    up = jnp.where(up <= block, up - 1, up)
    down = jnp.where(step >= block, step + 1, step)
    return jnp.where(2 * block < blocks, up, down) * NEAR + (place + i) % NEAR


def kernel(
    n,
    x_hbm,
    g_hbm,
    pi_hbm,
    po_hbm,
    ids_hbm,
    out_ref,
    x_buf,
    g_buf,
    pi_buf,
    po_buf,
    ids_ref,
    x_sum,
    g_sum,
    feat,
    recv,
    gram,
    parts,
    load_sem,
    ids_sem,
    send_a,
    recv_a,
    send_b,
    recv_b,
):
    me = lax.axis_index("row")
    quarter, mine = me // SLICES, me % SLICES
    chunks = x_buf.shape[1] // CHUNK

    barrier = pltpu.get_barrier_semaphore()
    for i in range(n - 1):
        pl.semaphore_signal(
            barrier, inc=1, device_id={"row": partner(me, n, i)}, device_id_type=MESH
        )

    ids_copy = pltpu.make_async_copy(ids_hbm, ids_ref, ids_sem)
    ids_copy.start()
    pairs = ((po_hbm, po_buf), (g_hbm, g_buf), (pi_hbm, pi_buf), (x_hbm, x_buf))

    def loads(c):
        cols = pl.ds(pl.multiple_of(c * CHUNK, CHUNK), CHUNK)
        return cols, [
            pltpu.make_async_copy(src.at[:, cols], dst.at[:, cols], load_sem.at[c, i])
            for i, (src, dst) in enumerate(pairs)
        ]

    @pl.loop(0, chunks)
    def _(c):
        for copy in loads(c)[1]:
            copy.start()

    g_sum[...] = jnp.zeros_like(g_sum)
    x_sum[...] = jnp.zeros_like(x_sum)

    @pl.loop(0, chunks)
    def _(c):
        cols, copies = loads(c)
        for copy in copies:
            copy.wait()
        g = dot_nt(po_buf[:, cols], g_buf[:, cols])
        x = dot_nt(pi_buf[:, cols], x_buf[:, cols])
        g_sum[...] += g
        x_sum[...] += x

    tokens = x_buf.shape[0]
    g = g_sum[...].astype(jnp.bfloat16).astype(jnp.float32)
    ids_copy.wait()
    ids = ids_ref[...].reshape(1, tokens)
    onehot = (ids == lax.broadcasted_iota(jnp.int32, (EX_DEV, tokens), 0)).astype(jnp.float32)
    masked = (g[:, None, :] * onehot[None, :, :]).reshape(RANK * EX_DEV, tokens)
    weighted = masked.astype(jnp.bfloat16)

    x = x_sum[...]
    outer = dot_nt(weighted, jnp.concatenate([x, x], axis=0).astype(jnp.bfloat16))
    half = RANK * EX_DEV // 2
    low = lax.broadcasted_iota(jnp.int32, (half, LANES), 1) < RANK
    packed = jnp.where(low, outer[:half], outer[half:]) * (1.0 / math.sqrt(TPE))
    feat[...] = packed.astype(jnp.bfloat16).reshape(feat.shape)

    pl.semaphore_wait(barrier, n - 1)
    for i in range(n - 1):
        target = partner(me, n, i)
        pltpu.make_async_remote_copy(
            src_ref=feat.at[lax.rem(target, SLICES)],
            dst_ref=recv.at[me],
            send_sem=send_a,
            recv_sem=recv_a,
            device_id={"row": target},
            device_id_type=MESH,
        ).start()
    recv[me] = feat[mine]
    rest = recv.at[pl.ds(0, n - 1)]
    pltpu.make_async_copy(rest, rest, recv_a).wait()

    def rows(block):
        block = block.astype(jnp.float32).reshape(-1, 2, EX_DEV, LANES)
        sides = [block[:, i].reshape(-1, LANES) for i in range(2)]
        return jnp.concatenate(sides, axis=1).astype(jnp.bfloat16)

    every = rows(recv[...])
    own = every if n == SLICES else rows(recv[pl.ds(quarter * SLICES, SLICES)])
    gram[...] = dot_nt(own, every).reshape(gram.shape)

    for i in range(SLICES - 1):
        to = partner(mine, SLICES, i)
        pltpu.make_async_remote_copy(
            src_ref=gram.at[to],
            dst_ref=parts.at[mine],
            send_sem=send_b,
            recv_sem=recv_b,
            device_id={"row": quarter * SLICES + to},
            device_id_type=MESH,
        ).start()
    parts[mine] = gram[mine]
    rest_b = parts.at[pl.ds(0, SLICES - 1)]
    pltpu.make_async_copy(rest_b, rest_b, recv_b).wait()
    out_ref[...] = jnp.sum(parts[...], axis=0) * (1.0 / RANK)
    pltpu.make_async_copy(rest, rest, send_a).wait()
    pltpu.make_async_copy(rest_b, rest_b, send_b).wait()


def shards(n, inputs, out_grads, proj_in, proj_out, example_ids):
    tokens, width = inputs.shape
    examples = EX_DEV * n
    hbm = pl.BlockSpec(memory_space=pl.ANY)
    vmem = pl.BlockSpec(memory_space=pltpu.VMEM)
    flops = 4 * tokens * width * RANK
    return pl.pallas_call(
        functools.partial(kernel, n),
        out_shape=pltpu.VMEM((EX_DEV, examples), jnp.float32),
        in_specs=[hbm] * 5,
        out_specs=vmem,
        scratch_shapes=[
            pltpu.VMEM((tokens, width), jnp.bfloat16),
            pltpu.VMEM((tokens, width), jnp.bfloat16),
            pltpu.VMEM((RANK, width), jnp.bfloat16),
            pltpu.VMEM((RANK, width), jnp.bfloat16),
            pltpu.VMEM((tokens,), jnp.int32),
            pltpu.VMEM((RANK, tokens), jnp.float32),
            pltpu.VMEM((RANK, tokens), jnp.float32),
            pltpu.VMEM((SLICES, 2 * EX_DEV, LANES), jnp.bfloat16),
            pltpu.VMEM((n, 2 * EX_DEV, LANES), jnp.bfloat16),
            pltpu.VMEM((SLICES, EX_DEV, examples), jnp.float32),
            pltpu.VMEM((SLICES, EX_DEV, examples), jnp.float32),
            pltpu.SemaphoreType.DMA((width // CHUNK, 4)),
            pltpu.SemaphoreType.DMA,
            pltpu.SemaphoreType.DMA,
            pltpu.SemaphoreType.DMA,
            pltpu.SemaphoreType.DMA,
            pltpu.SemaphoreType.DMA,
        ],
        compiler_params=pltpu.CompilerParams(
            collective_id=0, has_side_effects=True, vmem_limit_bytes=63 * 1024 * 1024
        ),
        cost_estimate=pl.CostEstimate(
            flops=flops, bytes_accessed=4 * (tokens + RANK) * width, transcendentals=0
        ),
    )(inputs, out_grads, proj_in.T, proj_out.T, example_ids)


def solution(mesh):
    in_specs = (P(("grp", "row"), None), P(("grp", "row"), None), P(), P(), P(("grp", "row")))
    out_specs = P(("grp", "row"), None)
    body = functools.partial(shards, mesh.shape["row"])
    return jax.shard_map(body, mesh=mesh, in_specs=in_specs, out_specs=out_specs, check_vma=False)
```

```python
import functools
import math

import jax
import jax.numpy as jnp
from jax import lax
from jax.experimental import pallas as pl
from jax.experimental.pallas import tpu as pltpu
from jax.sharding import PartitionSpec as P

RANK = 64
TPE = 32
EX_DEV = 8
LANES = 128
SLICES = 16
CHUNK = 1024
NEAR = 4
MESH = pl.DeviceIdType.MESH
NT = (((1,), (1,)), ((), ()))


def dot_nt(a, b):
    return lax.dot_general(a, b, NT, preferred_element_type=jnp.float32)


def partner(me, n, i):
    blocks = n // NEAR
    block, place = me // NEAR, me % NEAR
    if i >= n - NEAR:
        return block * NEAR + (place + 1 + i - (n - NEAR)) % NEAR
    step = i // NEAR
    up = blocks - 1 - step
    up = jnp.where(up <= block, up - 1, up)
    down = jnp.where(step >= block, step + 1, step)
    return jnp.where(2 * block < blocks, up, down) * NEAR + (place + i) % NEAR


def kernel(
    n,
    x_hbm,
    g_hbm,
    pi_hbm,
    po_hbm,
    ids_hbm,
    out_ref,
    x_buf,
    g_buf,
    pi_buf,
    po_buf,
    ids_ref,
    x_sum,
    g_sum,
    feat,
    recv,
    gram,
    parts,
    load_sem,
    ids_sem,
    send_a,
    recv_a,
    send_b,
    recv_b,
):
    me = lax.axis_index("row")
    quarter, mine = me // SLICES, me % SLICES
    chunks = x_buf.shape[1] // CHUNK

    barrier = pltpu.get_barrier_semaphore()
    for i in range(n - 1):
        pl.semaphore_signal(
            barrier, inc=1, device_id={"row": partner(me, n, i)}, device_id_type=MESH
        )

    ids_copy = pltpu.make_async_copy(ids_hbm, ids_ref, ids_sem)
    ids_copy.start()
    pairs = ((po_hbm, po_buf), (g_hbm, g_buf), (pi_hbm, pi_buf), (x_hbm, x_buf))

    def loads(c):
        cols = pl.ds(pl.multiple_of(c * CHUNK, CHUNK), CHUNK)
        return cols, [
            pltpu.make_async_copy(src.at[:, cols], dst.at[:, cols], load_sem.at[c, i])
            for i, (src, dst) in enumerate(pairs)
        ]

    @pl.loop(0, chunks)
    def _(c):
        for copy in loads(c)[1]:
            copy.start()

    g_sum[...] = jnp.zeros_like(g_sum)
    x_sum[...] = jnp.zeros_like(x_sum)

    @pl.loop(0, chunks)
    def _(c):
        cols, copies = loads(c)
        for copy in copies:
            copy.wait()
        g = dot_nt(po_buf[:, cols], g_buf[:, cols])
        x = dot_nt(x_buf[:, cols], pi_buf[:, cols])
        g_sum[...] += g
        x_sum[...] += x

    tokens = x_buf.shape[0]
    g = g_sum[...].astype(jnp.bfloat16).astype(jnp.float32)
    ids_copy.wait()
    ids = ids_ref[...].reshape(1, tokens)
    onehot = (ids == lax.broadcasted_iota(jnp.int32, (EX_DEV, tokens), 0)).astype(jnp.float32)
    masked = (g[:, None, :] * onehot[None, :, :]).reshape(RANK * EX_DEV, tokens)
    weighted = masked.astype(jnp.bfloat16)

    x = x_sum[...]
    x = jnp.concatenate([x, x], axis=1).astype(jnp.bfloat16)
    outer = jnp.dot(weighted, x, preferred_element_type=jnp.float32)
    half = RANK * EX_DEV // 2
    low = lax.broadcasted_iota(jnp.int32, (half, LANES), 1) < RANK
    packed = jnp.where(low, outer[:half], outer[half:]) * (1.0 / math.sqrt(TPE))
    feat[...] = packed.astype(jnp.bfloat16).reshape(feat.shape)

    pl.semaphore_wait(barrier, n - 1)
    for i in range(n - 1):
        target = partner(me, n, i)
        pltpu.make_async_remote_copy(
            src_ref=feat.at[lax.rem(target, SLICES)],
            dst_ref=recv.at[me],
            send_sem=send_a,
            recv_sem=recv_a,
            device_id={"row": target},
            device_id_type=MESH,
        ).start()
    recv[me] = feat[mine]
    rest = recv.at[pl.ds(0, n - 1)]
    pltpu.make_async_copy(rest, rest, recv_a).wait()

    def rows(block):
        block = block.astype(jnp.float32).reshape(-1, 2, EX_DEV, LANES)
        sides = [block[:, i].reshape(-1, LANES) for i in range(2)]
        return jnp.concatenate(sides, axis=1).astype(jnp.bfloat16)

    every = rows(recv[...])
    own = every if n == SLICES else rows(recv[pl.ds(quarter * SLICES, SLICES)])
    gram[...] = dot_nt(own, every).reshape(gram.shape)

    for i in range(SLICES - 1):
        to = partner(mine, SLICES, i)
        pltpu.make_async_remote_copy(
            src_ref=gram.at[to],
            dst_ref=parts.at[mine],
            send_sem=send_b,
            recv_sem=recv_b,
            device_id={"row": quarter * SLICES + to},
            device_id_type=MESH,
        ).start()
    parts[mine] = gram[mine]
    rest_b = parts.at[pl.ds(0, SLICES - 1)]
    pltpu.make_async_copy(rest_b, rest_b, recv_b).wait()
    out_ref[...] = jnp.sum(parts[...], axis=0) * (1.0 / RANK)
    pltpu.make_async_copy(rest, rest, send_a).wait()
    pltpu.make_async_copy(rest_b, rest_b, send_b).wait()


def shards(n, inputs, out_grads, proj_in, proj_out, example_ids):
    tokens, width = inputs.shape
    examples = EX_DEV * n
    hbm = pl.BlockSpec(memory_space=pl.ANY)
    vmem = pl.BlockSpec(memory_space=pltpu.VMEM)
    flops = 4 * tokens * width * RANK
    return pl.pallas_call(
        functools.partial(kernel, n),
        out_shape=pltpu.VMEM((EX_DEV, examples), jnp.float32),
        in_specs=[hbm] * 5,
        out_specs=vmem,
        scratch_shapes=[
            pltpu.VMEM((tokens, width), jnp.bfloat16),
            pltpu.VMEM((tokens, width), jnp.bfloat16),
            pltpu.VMEM((RANK, width), jnp.bfloat16),
            pltpu.VMEM((RANK, width), jnp.bfloat16),
            pltpu.VMEM((tokens,), jnp.int32),
            pltpu.VMEM((tokens, RANK), jnp.float32),
            pltpu.VMEM((RANK, tokens), jnp.float32),
            pltpu.VMEM((SLICES, 2 * EX_DEV, LANES), jnp.bfloat16),
            pltpu.VMEM((n, 2 * EX_DEV, LANES), jnp.bfloat16),
            pltpu.VMEM((SLICES, EX_DEV, examples), jnp.float32),
            pltpu.VMEM((SLICES, EX_DEV, examples), jnp.float32),
            pltpu.SemaphoreType.DMA((width // CHUNK, 4)),
            pltpu.SemaphoreType.DMA,
            pltpu.SemaphoreType.DMA,
            pltpu.SemaphoreType.DMA,
            pltpu.SemaphoreType.DMA,
            pltpu.SemaphoreType.DMA,
        ],
        compiler_params=pltpu.CompilerParams(
            collective_id=0, has_side_effects=True, vmem_limit_bytes=63 * 1024 * 1024
        ),
        cost_estimate=pl.CostEstimate(
            flops=flops, bytes_accessed=4 * (tokens + RANK) * width, transcendentals=0
        ),
    )(inputs, out_grads, proj_in.T, proj_out.T, example_ids)


def solution(mesh):
    in_specs = (P(("grp", "row"), None), P(("grp", "row"), None), P(), P(), P(("grp", "row")))
    out_specs = P(("grp", "row"), None)
    body = functools.partial(shards, mesh.shape["row"])
    return jax.shard_map(body, mesh=mesh, in_specs=in_specs, out_specs=out_specs, check_vma=False)
```

```python
import functools
import math

import jax
import jax.numpy as jnp
from jax import lax
from jax.experimental import pallas as pl
from jax.experimental.pallas import tpu as pltpu
from jax.sharding import PartitionSpec as P

RANK = 64
TPE = 32
EX_DEV = 8
LANES = 128
SLICES = 16
CHUNK = 1024
MESH = pl.DeviceIdType.MESH
NT = (((1,), (1,)), ((), ()))


def dot_nt(a, b):
    return lax.dot_general(a, b, NT, preferred_element_type=jnp.float32)


def partner(me, n, i):
    step = jnp.where(2 * me < n, 1, -1)
    return lax.rem(me + n + step * (n - 1 - i), n)


def kernel(
    n,
    x_hbm,
    g_hbm,
    pi_hbm,
    po_hbm,
    ids_hbm,
    out_ref,
    x_buf,
    g_buf,
    pi_buf,
    po_buf,
    ids_ref,
    x_sum,
    g_sum,
    feat,
    recv,
    gram,
    parts,
    load_sem,
    ids_sem,
    send_a,
    recv_a,
    send_b,
    recv_b,
):
    me = lax.axis_index("row")
    quarter, mine = me // SLICES, me % SLICES
    chunks = x_buf.shape[1] // CHUNK

    ids_copy = pltpu.make_async_copy(ids_hbm, ids_ref, ids_sem)
    ids_copy.start()
    pairs = ((po_hbm, po_buf), (g_hbm, g_buf), (pi_hbm, pi_buf), (x_hbm, x_buf))

    def loads(c):
        cols = pl.ds(pl.multiple_of(c * CHUNK, CHUNK), CHUNK)
        return cols, [
            pltpu.make_async_copy(src.at[:, cols], dst.at[:, cols], load_sem.at[c, i])
            for i, (src, dst) in enumerate(pairs)
        ]

    for copy in loads(0)[1]:
        copy.start()

    barrier = pltpu.get_barrier_semaphore()
    for i in range(n - 1):
        pl.semaphore_signal(
            barrier, inc=1, device_id={"row": partner(me, n, i)}, device_id_type=MESH
        )

    @pl.loop(1, chunks)
    def _(c):
        for copy in loads(c)[1]:
            copy.start()

    def project_g(c):
        cols, copies = loads(c)
        copies[0].wait()
        copies[1].wait()
        return lambda: dot_nt(po_buf[:, cols], g_buf[:, cols])

    def project_x(c):
        cols, copies = loads(c)
        copies[2].wait()
        copies[3].wait()
        return lambda: dot_nt(x_buf[:, cols], pi_buf[:, cols])

    g_sum[...] = project_g(0)()
    x_sum[...] = jnp.zeros_like(x_sum)

    @pl.loop(1, chunks)
    def _(c):
        x_part = project_x(c - 1)
        g_part = project_g(c)
        g, x = g_part(), x_part()
        g_sum[...] += g
        x_sum[...] += x

    ids_copy.wait()
    x = x_sum[...] + project_x(chunks - 1)()

    tokens = x_buf.shape[0]
    g = g_sum[...].astype(jnp.bfloat16).astype(jnp.float32)
    ids = ids_ref[...].reshape(1, tokens)
    onehot = (ids == lax.broadcasted_iota(jnp.int32, (EX_DEV, tokens), 0)).astype(jnp.float32)
    masked = (g[:, None, :] * onehot[None, :, :]).reshape(RANK * EX_DEV, tokens)
    weighted = masked.astype(jnp.bfloat16)

    x = jnp.concatenate([x, x], axis=1).astype(jnp.bfloat16)
    outer = jnp.dot(weighted, x, preferred_element_type=jnp.float32)
    half = RANK * EX_DEV // 2
    low = lax.broadcasted_iota(jnp.int32, (half, LANES), 1) < RANK
    packed = jnp.where(low, outer[:half], outer[half:]) * (1.0 / math.sqrt(TPE))
    feat[...] = packed.astype(jnp.bfloat16).reshape(feat.shape)

    pl.semaphore_wait(barrier, n - 1)
    for i in range(n - 1):
        target = partner(me, n, i)
        pltpu.make_async_remote_copy(
            src_ref=feat.at[lax.rem(target, SLICES)],
            dst_ref=recv.at[me],
            send_sem=send_a,
            recv_sem=recv_a,
            device_id={"row": target},
            device_id_type=MESH,
        ).start()
    recv[me] = feat[mine]
    rest = recv.at[pl.ds(0, n - 1)]
    pltpu.make_async_copy(rest, rest, recv_a).wait()

    def rows(block):
        block = block.astype(jnp.float32).reshape(-1, 2, EX_DEV, LANES)
        sides = [block[:, i].reshape(-1, LANES) for i in range(2)]
        return jnp.concatenate(sides, axis=1).astype(jnp.bfloat16)

    every = rows(recv[...])
    own = every if n == SLICES else rows(recv[pl.ds(quarter * SLICES, SLICES)])
    gram[...] = dot_nt(own, every).reshape(gram.shape)

    for i in range(SLICES - 1):
        to = partner(mine, SLICES, i)
        pltpu.make_async_remote_copy(
            src_ref=gram.at[to],
            dst_ref=parts.at[mine],
            send_sem=send_b,
            recv_sem=recv_b,
            device_id={"row": quarter * SLICES + to},
            device_id_type=MESH,
        ).start()
    parts[mine] = gram[mine]
    rest_b = parts.at[pl.ds(0, SLICES - 1)]
    pltpu.make_async_copy(rest_b, rest_b, recv_b).wait()
    out_ref[...] = jnp.sum(parts[...], axis=0) * (1.0 / RANK)
    pltpu.make_async_copy(rest, rest, send_a).wait()
    pltpu.make_async_copy(rest_b, rest_b, send_b).wait()


def shards(n, inputs, out_grads, proj_in, proj_out, example_ids):
    tokens, width = inputs.shape
    examples = EX_DEV * n
    hbm = pl.BlockSpec(memory_space=pl.ANY)
    vmem = pl.BlockSpec(memory_space=pltpu.VMEM)
    flops = 4 * tokens * width * RANK
    return pl.pallas_call(
        functools.partial(kernel, n),
        out_shape=pltpu.VMEM((EX_DEV, examples), jnp.float32),
        in_specs=[hbm] * 5,
        out_specs=vmem,
        scratch_shapes=[
            pltpu.VMEM((tokens, width), jnp.bfloat16),
            pltpu.VMEM((tokens, width), jnp.bfloat16),
            pltpu.VMEM((RANK, width), jnp.bfloat16),
            pltpu.VMEM((RANK, width), jnp.bfloat16),
            pltpu.VMEM((tokens,), jnp.int32),
            pltpu.VMEM((tokens, RANK), jnp.float32),
            pltpu.VMEM((RANK, tokens), jnp.float32),
            pltpu.VMEM((SLICES, 2 * EX_DEV, LANES), jnp.bfloat16),
            pltpu.VMEM((n, 2 * EX_DEV, LANES), jnp.bfloat16),
            pltpu.VMEM((SLICES, EX_DEV, examples), jnp.float32),
            pltpu.VMEM((SLICES, EX_DEV, examples), jnp.float32),
            pltpu.SemaphoreType.DMA((width // CHUNK, 4)),
            pltpu.SemaphoreType.DMA,
            pltpu.SemaphoreType.DMA,
            pltpu.SemaphoreType.DMA,
            pltpu.SemaphoreType.DMA,
            pltpu.SemaphoreType.DMA,
        ],
        compiler_params=pltpu.CompilerParams(
            collective_id=0, has_side_effects=True, vmem_limit_bytes=63 * 1024 * 1024
        ),
        cost_estimate=pl.CostEstimate(
            flops=flops, bytes_accessed=4 * (tokens + RANK) * width, transcendentals=0
        ),
    )(inputs, out_grads, proj_in.T, proj_out.T, example_ids)


def solution(mesh):
    in_specs = (P(("grp", "row"), None), P(("grp", "row"), None), P(), P(), P(("grp", "row")))
    out_specs = P(("grp", "row"), None)
    body = functools.partial(shards, mesh.shape["row"])
    return jax.shard_map(body, mesh=mesh, in_specs=in_specs, out_specs=out_specs, check_vma=False)
```

```python
import functools
import math

import jax
import jax.numpy as jnp
from jax import lax
from jax.experimental import pallas as pl
from jax.experimental.pallas import tpu as pltpu
from jax.sharding import PartitionSpec as P

RANK = 64
TPE = 32
EX_DEV = 8
LANES = 128
SLICES = 16
CHUNK = 1024
MESH = pl.DeviceIdType.MESH
NT = (((1,), (1,)), ((), ()))


def dot_nt(a, b):
    return lax.dot_general(a, b, NT, preferred_element_type=jnp.float32)


def partner(me, n, i):
    step = jnp.where(2 * me < n, 1, -1)
    return lax.rem(me + n + step * (n - 1 - i), n)


def kernel(
    n,
    x_hbm,
    g_hbm,
    pi_hbm,
    po_hbm,
    ids_hbm,
    out_ref,
    x_buf,
    g_buf,
    pi_buf,
    po_buf,
    ids_ref,
    x_sum,
    g_sum,
    feat,
    recv,
    gram,
    parts,
    load_sem,
    ids_sem,
    send_a,
    recv_a,
    send_b,
    recv_b,
):
    me = lax.axis_index("row")
    quarter, mine = me // SLICES, me % SLICES
    chunks = x_buf.shape[1] // CHUNK

    ids_copy = pltpu.make_async_copy(ids_hbm, ids_ref, ids_sem)
    ids_copy.start()
    pairs = ((po_hbm, po_buf), (g_hbm, g_buf), (pi_hbm, pi_buf), (x_hbm, x_buf))

    def loads(c):
        cols = pl.ds(pl.multiple_of(c * CHUNK, CHUNK), CHUNK)
        return cols, [
            pltpu.make_async_copy(src.at[:, cols], dst.at[:, cols], load_sem.at[c, i])
            for i, (src, dst) in enumerate(pairs)
        ]

    for copy in loads(0)[1]:
        copy.start()

    barrier = pltpu.get_barrier_semaphore()
    @pl.loop(0, n - 1)
    def _(i):
        pl.semaphore_signal(
            barrier, inc=1, device_id={"row": partner(me, n, i)}, device_id_type=MESH
        )

    @pl.loop(1, chunks)
    def _(c):
        for copy in loads(c)[1]:
            copy.start()

    def project_g(c):
        cols, copies = loads(c)
        copies[0].wait()
        copies[1].wait()
        return lambda: dot_nt(po_buf[:, cols], g_buf[:, cols])

    def project_x(c):
        cols, copies = loads(c)
        copies[2].wait()
        copies[3].wait()
        return lambda: dot_nt(x_buf[:, cols], pi_buf[:, cols])

    g_sum[...] = project_g(0)()
    x_sum[...] = jnp.zeros_like(x_sum)

    @pl.loop(1, chunks)
    def _(c):
        x_part = project_x(c - 1)
        g_part = project_g(c)
        g, x = g_part(), x_part()
        g_sum[...] += g
        x_sum[...] += x

    ids_copy.wait()
    x = x_sum[...] + project_x(chunks - 1)()

    tokens = x_buf.shape[0]
    g = g_sum[...].astype(jnp.bfloat16).astype(jnp.float32)
    ids = ids_ref[...].reshape(1, tokens)
    onehot = (ids == lax.broadcasted_iota(jnp.int32, (EX_DEV, tokens), 0)).astype(jnp.float32)
    masked = (g[:, None, :] * onehot[None, :, :]).reshape(RANK * EX_DEV, tokens)
    weighted = masked.astype(jnp.bfloat16)

    x = jnp.concatenate([x, x], axis=1).astype(jnp.bfloat16)
    outer = jnp.dot(weighted, x, preferred_element_type=jnp.float32)
    half = RANK * EX_DEV // 2
    low = lax.broadcasted_iota(jnp.int32, (half, LANES), 1) < RANK
    packed = jnp.where(low, outer[:half], outer[half:]) * (1.0 / math.sqrt(TPE))
    feat[...] = packed.astype(jnp.bfloat16).reshape(feat.shape)

    pl.semaphore_wait(barrier, n - 1)
    @pl.loop(0, n - 1)
    def _(i):
        target = partner(me, n, i)
        pltpu.make_async_remote_copy(
            src_ref=feat.at[lax.rem(target, SLICES)],
            dst_ref=recv.at[me],
            send_sem=send_a,
            recv_sem=recv_a,
            device_id={"row": target},
            device_id_type=MESH,
        ).start()

    recv[me] = feat[mine]
    rest = recv.at[pl.ds(0, n - 1)]
    pltpu.make_async_copy(rest, rest, recv_a).wait()

    def rows(block):
        block = block.astype(jnp.float32).reshape(-1, 2, EX_DEV, LANES)
        sides = [block[:, i].reshape(-1, LANES) for i in range(2)]
        return jnp.concatenate(sides, axis=1).astype(jnp.bfloat16)

    every = rows(recv[...])
    own = every if n == SLICES else rows(recv[pl.ds(quarter * SLICES, SLICES)])
    gram[...] = dot_nt(own, every).reshape(gram.shape)

    @pl.loop(0, SLICES - 1)
    def _(i):
        to = partner(mine, SLICES, i)
        pltpu.make_async_remote_copy(
            src_ref=gram.at[to],
            dst_ref=parts.at[mine],
            send_sem=send_b,
            recv_sem=recv_b,
            device_id={"row": quarter * SLICES + to},
            device_id_type=MESH,
        ).start()

    parts[mine] = gram[mine]
    rest_b = parts.at[pl.ds(0, SLICES - 1)]
    pltpu.make_async_copy(rest_b, rest_b, recv_b).wait()
    out_ref[...] = jnp.sum(parts[...], axis=0) * (1.0 / RANK)
    pltpu.make_async_copy(rest, rest, send_a).wait()
    pltpu.make_async_copy(rest_b, rest_b, send_b).wait()


def shards(n, inputs, out_grads, proj_in, proj_out, example_ids):
    tokens, width = inputs.shape
    examples = EX_DEV * n
    hbm = pl.BlockSpec(memory_space=pl.ANY)
    vmem = pl.BlockSpec(memory_space=pltpu.VMEM)
    flops = 4 * tokens * width * RANK
    return pl.pallas_call(
        functools.partial(kernel, n),
        out_shape=pltpu.VMEM((EX_DEV, examples), jnp.float32),
        in_specs=[hbm] * 5,
        out_specs=vmem,
        scratch_shapes=[
            pltpu.VMEM((tokens, width), jnp.bfloat16),
            pltpu.VMEM((tokens, width), jnp.bfloat16),
            pltpu.VMEM((RANK, width), jnp.bfloat16),
            pltpu.VMEM((RANK, width), jnp.bfloat16),
            pltpu.VMEM((tokens,), jnp.int32),
            pltpu.VMEM((tokens, RANK), jnp.float32),
            pltpu.VMEM((RANK, tokens), jnp.float32),
            pltpu.VMEM((SLICES, 2 * EX_DEV, LANES), jnp.bfloat16),
            pltpu.VMEM((n, 2 * EX_DEV, LANES), jnp.bfloat16),
            pltpu.VMEM((SLICES, EX_DEV, examples), jnp.float32),
            pltpu.VMEM((SLICES, EX_DEV, examples), jnp.float32),
            pltpu.SemaphoreType.DMA((width // CHUNK, 4)),
            pltpu.SemaphoreType.DMA,
            pltpu.SemaphoreType.DMA,
            pltpu.SemaphoreType.DMA,
            pltpu.SemaphoreType.DMA,
            pltpu.SemaphoreType.DMA,
        ],
        compiler_params=pltpu.CompilerParams(
            collective_id=0, has_side_effects=True, vmem_limit_bytes=63 * 1024 * 1024
        ),
        cost_estimate=pl.CostEstimate(
            flops=flops, bytes_accessed=4 * (tokens + RANK) * width, transcendentals=0
        ),
    )(inputs, out_grads, proj_in.T, proj_out.T, example_ids)


def solution(mesh):
    in_specs = (P(("grp", "row"), None), P(("grp", "row"), None), P(), P(), P(("grp", "row")))
    out_specs = P(("grp", "row"), None)
    body = functools.partial(shards, mesh.shape["row"])
    return jax.shard_map(body, mesh=mesh, in_specs=in_specs, out_specs=out_specs, check_vma=False)
```

```python
import functools
import math

import jax
import jax.numpy as jnp
from jax import lax
from jax.experimental import pallas as pl
from jax.experimental.pallas import tpu as pltpu
from jax.sharding import PartitionSpec as P

RANK = 64
TPE = 32
EX_DEV = 8
LANES = 128
SLICES = 16
CHUNK = 1024
NEAR = 4
PAIR = 2
MESH = pl.DeviceIdType.MESH
NT = (((1,), (1,)), ((), ()))


def dot_nt(a, b):
    return lax.dot_general(a, b, NT, preferred_element_type=jnp.float32)


def partner(me, n, i):
    blocks = n // NEAR
    block, place = lax.div(me, NEAR), lax.rem(me, NEAR)
    if i >= n - NEAR:
        return block * NEAR + lax.rem(place + 1 + i - (n - NEAR), NEAR)
    step = i // NEAR
    up = blocks - 1 - step
    up = jnp.where(up <= block, up - 1, up)
    down = jnp.where(step >= block, step + 1, step)
    return jnp.where(2 * block < blocks, up, down) * NEAR + lax.rem(place + i, NEAR)


def kernel(
    n,
    x_hbm,
    g_hbm,
    pi_hbm,
    po_hbm,
    ids_hbm,
    out_ref,
    x_buf,
    g_buf,
    pi_buf,
    po_buf,
    ids_ref,
    x_sum,
    g_sum,
    feat,
    recv,
    gram,
    swapped,
    sums,
    parts,
    load_sem,
    ids_sem,
    send_a,
    recv_a,
    swap_sem,
    send_b,
    recv_b,
):
    me = lax.axis_index("row")
    quarter, mine = me // SLICES, me % SLICES
    chunks = x_buf.shape[1] // CHUNK

    ids_copy = pltpu.make_async_copy(ids_hbm, ids_ref, ids_sem)
    ids_copy.start()
    pairs = ((po_hbm, po_buf), (g_hbm, g_buf), (pi_hbm, pi_buf), (x_hbm, x_buf))

    def loads(c):
        cols = pl.ds(pl.multiple_of(c * CHUNK, CHUNK), CHUNK)
        return cols, [
            pltpu.make_async_copy(src.at[:, cols], dst.at[:, cols], load_sem.at[c, i])
            for i, (src, dst) in enumerate(pairs)
        ]

    for copy in loads(0)[1]:
        copy.start()

    barrier = pltpu.get_barrier_semaphore()
    for i in range(n - 1):
        pl.semaphore_signal(
            barrier, inc=1, device_id={"row": partner(me, n, i)}, device_id_type=MESH
        )

    @pl.loop(1, chunks)
    def _(c):
        for copy in loads(c)[1]:
            copy.start()

    def project_g(c):
        cols, copies = loads(c)
        copies[0].wait()
        copies[1].wait()
        return lambda: dot_nt(po_buf[:, cols], g_buf[:, cols])

    def project_x(c):
        cols, copies = loads(c)
        copies[2].wait()
        copies[3].wait()
        return lambda: dot_nt(x_buf[:, cols], pi_buf[:, cols])

    g_sum[...] = project_g(0)()
    x_sum[...] = jnp.zeros_like(x_sum)

    @pl.loop(1, chunks)
    def _(c):
        x_part = project_x(c - 1)
        g_part = project_g(c)
        g, x = g_part(), x_part()
        g_sum[...] += g
        x_sum[...] += x

    ids_copy.wait()
    x = x_sum[...] + project_x(chunks - 1)()

    tokens = x_buf.shape[0]
    g = g_sum[...].astype(jnp.bfloat16).astype(jnp.float32)
    ids = ids_ref[...].reshape(1, tokens)
    onehot = (ids == lax.broadcasted_iota(jnp.int32, (EX_DEV, tokens), 0)).astype(jnp.float32)
    masked = (g[:, None, :] * onehot[None, :, :]).reshape(RANK * EX_DEV, tokens)
    weighted = masked.astype(jnp.bfloat16)

    x = jnp.concatenate([x, x], axis=1).astype(jnp.bfloat16)
    outer = jnp.dot(weighted, x, preferred_element_type=jnp.float32)
    half = RANK * EX_DEV // 2
    low = lax.broadcasted_iota(jnp.int32, (half, LANES), 1) < RANK
    packed = jnp.where(low, outer[:half], outer[half:]) * (1.0 / math.sqrt(TPE))
    feat[...] = packed.astype(jnp.bfloat16).reshape(feat.shape)

    pl.semaphore_wait(barrier, n - 1)
    for i in range(n - 1):
        target = partner(me, n, i)
        pltpu.make_async_remote_copy(
            src_ref=feat.at[lax.rem(target, SLICES)],
            dst_ref=recv.at[me],
            send_sem=send_a,
            recv_sem=recv_a,
            device_id={"row": target},
            device_id_type=MESH,
        ).start()

    recv[me] = feat[mine]
    rest = recv.at[pl.ds(0, n - 1)]
    pltpu.make_async_copy(rest, rest, recv_a).wait()

    def rows(block):
        block = block.astype(jnp.float32).reshape(-1, 2, EX_DEV, LANES)
        sides = [block[:, i].reshape(-1, LANES) for i in range(2)]
        return jnp.concatenate(sides, axis=1).astype(jnp.bfloat16)

    every = rows(recv[...])
    own = every if n == SLICES else rows(recv[pl.ds(quarter * SLICES, SLICES)])
    products = dot_nt(own, every).reshape(-1, PAIR, EX_DEV, every.shape[0])
    for core in range(PAIR):
        gram[core] = products[:, core]

    chips = SLICES // PAIR
    chip, side = lax.div(mine, PAIR), lax.rem(mine, PAIR)
    swap = pltpu.make_async_remote_copy(
        src_ref=gram.at[1 - side],
        dst_ref=swapped,
        send_sem=swap_sem.at[0],
        recv_sem=swap_sem.at[1],
        device_id={"row": me + 1 - 2 * side},
        device_id_type=MESH,
    )
    swap.start()
    swap.wait_recv()
    sums[...] = gram[side] + swapped[...]

    for i in range(chips - 1):
        to = partner(chip, chips, i)
        pltpu.make_async_remote_copy(
            src_ref=sums.at[to],
            dst_ref=parts.at[chip],
            send_sem=send_b,
            recv_sem=recv_b,
            device_id={"row": quarter * SLICES + to * PAIR + side},
            device_id_type=MESH,
        ).start()
    parts[chip] = sums[chip]
    rest_b = parts.at[pl.ds(0, chips - 1)]
    pltpu.make_async_copy(rest_b, rest_b, recv_b).wait()
    out_ref[...] = jnp.sum(parts[...], axis=0) * (1.0 / RANK)
    swap.wait_send()
    pltpu.make_async_copy(rest, rest, send_a).wait()
    pltpu.make_async_copy(rest_b, rest_b, send_b).wait()


def shards(n, inputs, out_grads, proj_in, proj_out, example_ids):
    tokens, width = inputs.shape
    examples = EX_DEV * n
    hbm = pl.BlockSpec(memory_space=pl.ANY)
    vmem = pl.BlockSpec(memory_space=pltpu.VMEM)
    flops = 4 * tokens * width * RANK
    return pl.pallas_call(
        functools.partial(kernel, n),
        out_shape=pltpu.VMEM((EX_DEV, examples), jnp.float32),
        in_specs=[hbm] * 5,
        out_specs=vmem,
        scratch_shapes=[
            pltpu.VMEM((tokens, width), jnp.bfloat16),
            pltpu.VMEM((tokens, width), jnp.bfloat16),
            pltpu.VMEM((RANK, width), jnp.bfloat16),
            pltpu.VMEM((RANK, width), jnp.bfloat16),
            pltpu.VMEM((tokens,), jnp.int32),
            pltpu.VMEM((tokens, RANK), jnp.float32),
            pltpu.VMEM((RANK, tokens), jnp.float32),
            pltpu.VMEM((SLICES, 2 * EX_DEV, LANES), jnp.bfloat16),
            pltpu.VMEM((n, 2 * EX_DEV, LANES), jnp.bfloat16),
            pltpu.VMEM((PAIR, SLICES // PAIR, EX_DEV, examples), jnp.float32),
            pltpu.VMEM((SLICES // PAIR, EX_DEV, examples), jnp.float32),
            pltpu.VMEM((SLICES // PAIR, EX_DEV, examples), jnp.float32),
            pltpu.VMEM((SLICES // PAIR, EX_DEV, examples), jnp.float32),
            pltpu.SemaphoreType.DMA((width // CHUNK, 4)),
            pltpu.SemaphoreType.DMA,
            pltpu.SemaphoreType.DMA,
            pltpu.SemaphoreType.DMA,
            pltpu.SemaphoreType.DMA((2,)),
            pltpu.SemaphoreType.DMA,
            pltpu.SemaphoreType.DMA,
        ],
        compiler_params=pltpu.CompilerParams(
            collective_id=0, has_side_effects=True, vmem_limit_bytes=63 * 1024 * 1024
        ),
        cost_estimate=pl.CostEstimate(
            flops=flops, bytes_accessed=4 * (tokens + RANK) * width, transcendentals=0
        ),
    )(inputs, out_grads, proj_in.T, proj_out.T, example_ids)


def solution(mesh):
    in_specs = (P(("grp", "row"), None), P(("grp", "row"), None), P(), P(), P(("grp", "row")))
    out_specs = P(("grp", "row"), None)
    body = functools.partial(shards, mesh.shape["row"])
    return jax.shard_map(body, mesh=mesh, in_specs=in_specs, out_specs=out_specs, check_vma=False)
```

```python
import functools
import math

import jax
import jax.numpy as jnp
from jax import lax
from jax.experimental import pallas as pl
from jax.experimental.pallas import tpu as pltpu
from jax.sharding import PartitionSpec as P

RANK = 64
TPE = 32
EX_DEV = 8
LANES = 128
SLICES = 16
CHUNK = 2048
NEAR = 4
MESH = pl.DeviceIdType.MESH
NT = (((1,), (1,)), ((), ()))


def dot_nt(a, b):
    return lax.dot_general(a, b, NT, preferred_element_type=jnp.float32)


def partner(me, n, i):
    blocks = n // NEAR
    block, place = lax.div(me, NEAR), lax.rem(me, NEAR)
    if i >= n - NEAR:
        return block * NEAR + lax.rem(place + 1 + i - (n - NEAR), NEAR)
    step = i // NEAR
    up = blocks - 1 - step
    up = jnp.where(up <= block, up - 1, up)
    down = jnp.where(step >= block, step + 1, step)
    return jnp.where(2 * block < blocks, up, down) * NEAR + lax.rem(place + i, NEAR)


def kernel(
    n,
    x_hbm,
    g_hbm,
    pi_hbm,
    po_hbm,
    ids_hbm,
    out_ref,
    x_buf,
    g_buf,
    pi_buf,
    po_buf,
    ids_ref,
    x_sum,
    g_sum,
    feat,
    recv,
    gram,
    parts,
    load_sem,
    ids_sem,
    send_a,
    recv_a,
    send_b,
    recv_b,
):
    me = lax.axis_index("row")
    quarter, mine = me // SLICES, me % SLICES
    chunks = x_buf.shape[1] // CHUNK

    ids_copy = pltpu.make_async_copy(ids_hbm, ids_ref, ids_sem)
    ids_copy.start()
    pairs = ((po_hbm, po_buf), (g_hbm, g_buf), (pi_hbm, pi_buf), (x_hbm, x_buf))

    def loads(c):
        cols = pl.ds(pl.multiple_of(c * CHUNK, CHUNK), CHUNK)
        return cols, [
            pltpu.make_async_copy(src.at[:, cols], dst.at[:, cols], load_sem.at[c, i])
            for i, (src, dst) in enumerate(pairs)
        ]

    for copy in loads(0)[1]:
        copy.start()

    barrier = pltpu.get_barrier_semaphore()
    for i in range(n - 1):
        pl.semaphore_signal(
            barrier, inc=1, device_id={"row": partner(me, n, i)}, device_id_type=MESH
        )

    @pl.loop(1, chunks)
    def _(c):
        for copy in loads(c)[1]:
            copy.start()

    g_sum[...] = jnp.zeros_like(g_sum)
    x_sum[...] = jnp.zeros_like(x_sum)

    @pl.loop(0, chunks)
    def _(c):
        cols, copies = loads(c)
        for copy in copies:
            copy.wait()
        g = dot_nt(po_buf[:, cols], g_buf[:, cols])
        x = dot_nt(x_buf[:, cols], pi_buf[:, cols])
        g_sum[...] += g
        x_sum[...] += x

    tokens = x_buf.shape[0]
    g = g_sum[...].astype(jnp.bfloat16).astype(jnp.float32)
    ids_copy.wait()
    ids = ids_ref[...].reshape(1, tokens)
    onehot = (ids == lax.broadcasted_iota(jnp.int32, (EX_DEV, tokens), 0)).astype(jnp.float32)
    masked = (g[:, None, :] * onehot[None, :, :]).reshape(RANK * EX_DEV, tokens)
    weighted = masked.astype(jnp.bfloat16)

    x = x_sum[...]
    x = jnp.concatenate([x, x], axis=1).astype(jnp.bfloat16)
    outer = jnp.dot(weighted, x, preferred_element_type=jnp.float32)
    half = RANK * EX_DEV // 2
    low = lax.broadcasted_iota(jnp.int32, (half, LANES), 1) < RANK
    packed = jnp.where(low, outer[:half], outer[half:]) * (1.0 / math.sqrt(TPE))
    feat[...] = packed.astype(jnp.bfloat16).reshape(feat.shape)

    pl.semaphore_wait(barrier, n - 1)
    for i in range(n - 1):
        target = partner(me, n, i)
        pltpu.make_async_remote_copy(
            src_ref=feat.at[lax.rem(target, SLICES)],
            dst_ref=recv.at[me],
            send_sem=send_a,
            recv_sem=recv_a,
            device_id={"row": target},
            device_id_type=MESH,
        ).start()
    recv[me] = feat[mine]
    rest = recv.at[pl.ds(0, n - 1)]
    pltpu.make_async_copy(rest, rest, recv_a).wait()

    def rows(block):
        block = block.astype(jnp.float32).reshape(-1, 2, EX_DEV, LANES)
        sides = [block[:, i].reshape(-1, LANES) for i in range(2)]
        return jnp.concatenate(sides, axis=1).astype(jnp.bfloat16)

    every = rows(recv[...])
    own = every if n == SLICES else rows(recv[pl.ds(quarter * SLICES, SLICES)])
    gram[...] = dot_nt(own, every).reshape(gram.shape)

    for i in range(SLICES - 1):
        to = partner(mine, SLICES, i)
        pltpu.make_async_remote_copy(
            src_ref=gram.at[to],
            dst_ref=parts.at[mine],
            send_sem=send_b,
            recv_sem=recv_b,
            device_id={"row": quarter * SLICES + to},
            device_id_type=MESH,
        ).start()
    parts[mine] = gram[mine]
    rest_b = parts.at[pl.ds(0, SLICES - 1)]
    pltpu.make_async_copy(rest_b, rest_b, recv_b).wait()
    out_ref[...] = jnp.sum(parts[...], axis=0) * (1.0 / RANK)
    pltpu.make_async_copy(rest, rest, send_a).wait()
    pltpu.make_async_copy(rest_b, rest_b, send_b).wait()


def shards(n, inputs, out_grads, proj_in, proj_out, example_ids):
    tokens, width = inputs.shape
    examples = EX_DEV * n
    hbm = pl.BlockSpec(memory_space=pl.ANY)
    vmem = pl.BlockSpec(memory_space=pltpu.VMEM)
    flops = 4 * tokens * width * RANK
    return pl.pallas_call(
        functools.partial(kernel, n),
        out_shape=pltpu.VMEM((EX_DEV, examples), jnp.float32),
        in_specs=[hbm] * 5,
        out_specs=vmem,
        scratch_shapes=[
            pltpu.VMEM((tokens, width), jnp.bfloat16),
            pltpu.VMEM((tokens, width), jnp.bfloat16),
            pltpu.VMEM((RANK, width), jnp.bfloat16),
            pltpu.VMEM((RANK, width), jnp.bfloat16),
            pltpu.VMEM((tokens,), jnp.int32),
            pltpu.VMEM((tokens, RANK), jnp.float32),
            pltpu.VMEM((RANK, tokens), jnp.float32),
            pltpu.VMEM((SLICES, 2 * EX_DEV, LANES), jnp.bfloat16),
            pltpu.VMEM((n, 2 * EX_DEV, LANES), jnp.bfloat16),
            pltpu.VMEM((SLICES, EX_DEV, examples), jnp.float32),
            pltpu.VMEM((SLICES, EX_DEV, examples), jnp.float32),
            pltpu.SemaphoreType.DMA((width // CHUNK, 4)),
            pltpu.SemaphoreType.DMA,
            pltpu.SemaphoreType.DMA,
            pltpu.SemaphoreType.DMA,
            pltpu.SemaphoreType.DMA,
            pltpu.SemaphoreType.DMA,
        ],
        compiler_params=pltpu.CompilerParams(
            collective_id=0, has_side_effects=True, vmem_limit_bytes=63 * 1024 * 1024
        ),
        cost_estimate=pl.CostEstimate(
            flops=flops, bytes_accessed=4 * (tokens + RANK) * width, transcendentals=0
        ),
    )(inputs, out_grads, proj_in.T, proj_out.T, example_ids)


def solution(mesh):
    in_specs = (P(("grp", "row"), None), P(("grp", "row"), None), P(), P(), P(("grp", "row")))
    out_specs = P(("grp", "row"), None)
    body = functools.partial(shards, mesh.shape["row"])
    return jax.shard_map(body, mesh=mesh, in_specs=in_specs, out_specs=out_specs, check_vma=False)
```

```python
import functools
import math

import jax
import jax.numpy as jnp
from jax import lax
from jax.experimental import pallas as pl
from jax.experimental.pallas import tpu as pltpu
from jax.sharding import PartitionSpec as P

RANK = 64
TPE = 32
EX_DEV = 8
LANES = 128
SLICES = 16
CHUNK = 2048
NEAR = 4
MESH = pl.DeviceIdType.MESH
NT = (((1,), (1,)), ((), ()))


def dot_nt(a, b):
    return lax.dot_general(a, b, NT, preferred_element_type=jnp.float32)


def partner(me, n, i):
    blocks = n // NEAR
    block, place = lax.div(me, NEAR), lax.rem(me, NEAR)
    if i >= n - NEAR:
        return block * NEAR + lax.rem(place + 1 + i - (n - NEAR), NEAR)
    step = i // NEAR
    up = blocks - 1 - step
    up = jnp.where(up <= block, up - 1, up)
    down = jnp.where(step >= block, step + 1, step)
    return jnp.where(2 * block < blocks, up, down) * NEAR + lax.rem(place + i, NEAR)


def kernel(
    n,
    x_hbm,
    g_hbm,
    pi_hbm,
    po_hbm,
    ids_hbm,
    out_ref,
    x_buf,
    g_buf,
    pi_buf,
    po_buf,
    ids_ref,
    x_sum,
    g_sum,
    feat,
    recv,
    gram,
    parts,
    load_sem,
    ids_sem,
    send_a,
    recv_a,
    send_b,
    recv_b,
):
    me = lax.axis_index("row")
    quarter, mine = me // SLICES, me % SLICES
    chunks = x_buf.shape[1] // CHUNK

    ids_copy = pltpu.make_async_copy(ids_hbm, ids_ref, ids_sem)
    ids_copy.start()
    pairs = ((po_hbm, po_buf), (g_hbm, g_buf), (pi_hbm, pi_buf), (x_hbm, x_buf))

    def loads(c):
        cols = pl.ds(pl.multiple_of(c * CHUNK, CHUNK), CHUNK)
        return cols, [
            pltpu.make_async_copy(src.at[:, cols], dst.at[:, cols], load_sem.at[c, i])
            for i, (src, dst) in enumerate(pairs)
        ]

    for copy in loads(0)[1]:
        copy.start()

    barrier = pltpu.get_barrier_semaphore()
    for i in range(n - 1):
        pl.semaphore_signal(
            barrier, inc=1, device_id={"row": partner(me, n, i)}, device_id_type=MESH
        )

    @pl.loop(1, chunks)
    def _(c):
        for copy in loads(c)[1]:
            copy.start()

    g_sum[...] = jnp.zeros_like(g_sum)
    x_sum[...] = jnp.zeros_like(x_sum)

    @pl.loop(0, chunks)
    def _(c):
        cols, copies = loads(c)
        for copy in copies:
            copy.wait()
        g = dot_nt(po_buf[:, cols], g_buf[:, cols])
        x = dot_nt(x_buf[:, cols], pi_buf[:, cols])
        g_sum[...] += g
        x_sum[...] += x

    pl.semaphore_wait(barrier, n - 1)

    tokens = x_buf.shape[0]
    g = g_sum[...].astype(jnp.bfloat16).astype(jnp.float32)
    ids_copy.wait()
    ids = ids_ref[...].reshape(1, tokens)
    onehot = (ids == lax.broadcasted_iota(jnp.int32, (EX_DEV, tokens), 0)).astype(jnp.float32)
    masked = (g[:, None, :] * onehot[None, :, :]).reshape(RANK * EX_DEV, tokens)
    weighted = masked.astype(jnp.bfloat16)

    x = x_sum[...]
    x = jnp.concatenate([x, x], axis=1).astype(jnp.bfloat16)
    outer = jnp.dot(weighted, x, preferred_element_type=jnp.float32)
    half = RANK * EX_DEV // 2
    low = lax.broadcasted_iota(jnp.int32, (half, LANES), 1) < RANK
    packed = jnp.where(low, outer[:half], outer[half:]) * (1.0 / math.sqrt(TPE))
    feat[...] = packed.astype(jnp.bfloat16).reshape(feat.shape)

    for i in range(n - 1):
        target = partner(me, n, i)
        pltpu.make_async_remote_copy(
            src_ref=feat.at[lax.rem(target, SLICES)],
            dst_ref=recv.at[me],
            send_sem=send_a,
            recv_sem=recv_a,
            device_id={"row": target},
            device_id_type=MESH,
        ).start()
    recv[me] = feat[mine]
    rest = recv.at[pl.ds(0, n - 1)]
    pltpu.make_async_copy(rest, rest, recv_a).wait()

    def rows(block):
        block = block.astype(jnp.float32).reshape(-1, 2, EX_DEV, LANES)
        sides = [block[:, i].reshape(-1, LANES) for i in range(2)]
        return jnp.concatenate(sides, axis=1).astype(jnp.bfloat16)

    every = rows(recv[...])
    own = every if n == SLICES else rows(recv[pl.ds(quarter * SLICES, SLICES)])
    gram[...] = dot_nt(own, every).reshape(gram.shape)

    for i in range(SLICES - 1):
        to = partner(mine, SLICES, i)
        pltpu.make_async_remote_copy(
            src_ref=gram.at[to],
            dst_ref=parts.at[mine],
            send_sem=send_b,
            recv_sem=recv_b,
            device_id={"row": quarter * SLICES + to},
            device_id_type=MESH,
        ).start()
    parts[mine] = gram[mine]
    rest_b = parts.at[pl.ds(0, SLICES - 1)]
    pltpu.make_async_copy(rest_b, rest_b, recv_b).wait()
    out_ref[...] = jnp.sum(parts[...], axis=0) * (1.0 / RANK)
    pltpu.make_async_copy(rest, rest, send_a).wait()
    pltpu.make_async_copy(rest_b, rest_b, send_b).wait()


def shards(n, inputs, out_grads, proj_in, proj_out, example_ids):
    tokens, width = inputs.shape
    examples = EX_DEV * n
    hbm = pl.BlockSpec(memory_space=pl.ANY)
    vmem = pl.BlockSpec(memory_space=pltpu.VMEM)
    flops = 4 * tokens * width * RANK
    return pl.pallas_call(
        functools.partial(kernel, n),
        out_shape=pltpu.VMEM((EX_DEV, examples), jnp.float32),
        in_specs=[hbm] * 5,
        out_specs=vmem,
        scratch_shapes=[
            pltpu.VMEM((tokens, width), jnp.bfloat16),
            pltpu.VMEM((tokens, width), jnp.bfloat16),
            pltpu.VMEM((RANK, width), jnp.bfloat16),
            pltpu.VMEM((RANK, width), jnp.bfloat16),
            pltpu.VMEM((tokens,), jnp.int32),
            pltpu.VMEM((tokens, RANK), jnp.float32),
            pltpu.VMEM((RANK, tokens), jnp.float32),
            pltpu.VMEM((SLICES, 2 * EX_DEV, LANES), jnp.bfloat16),
            pltpu.VMEM((n, 2 * EX_DEV, LANES), jnp.bfloat16),
            pltpu.VMEM((SLICES, EX_DEV, examples), jnp.float32),
            pltpu.VMEM((SLICES, EX_DEV, examples), jnp.float32),
            pltpu.SemaphoreType.DMA((width // CHUNK, 4)),
            pltpu.SemaphoreType.DMA,
            pltpu.SemaphoreType.DMA,
            pltpu.SemaphoreType.DMA,
            pltpu.SemaphoreType.DMA,
            pltpu.SemaphoreType.DMA,
        ],
        compiler_params=pltpu.CompilerParams(
            collective_id=0, has_side_effects=True, vmem_limit_bytes=63 * 1024 * 1024
        ),
        cost_estimate=pl.CostEstimate(
            flops=flops, bytes_accessed=4 * (tokens + RANK) * width, transcendentals=0
        ),
    )(inputs, out_grads, proj_in.T, proj_out.T, example_ids)


def solution(mesh):
    in_specs = (P(("grp", "row"), None), P(("grp", "row"), None), P(), P(), P(("grp", "row")))
    out_specs = P(("grp", "row"), None)
    body = functools.partial(shards, mesh.shape["row"])
    return jax.shard_map(body, mesh=mesh, in_specs=in_specs, out_specs=out_specs, check_vma=False)
```

```python
import functools
import math

import jax
import jax.numpy as jnp
from jax import lax
from jax.experimental import pallas as pl
from jax.experimental.pallas import tpu as pltpu
from jax.sharding import PartitionSpec as P

RANK = 64
TPE = 32
EX_DEV = 8
LANES = 128
SLICES = 16
CHUNK = 2048
NEAR = 4
MESH = pl.DeviceIdType.MESH
NT = (((1,), (1,)), ((), ()))


def dot_nt(a, b):
    return lax.dot_general(a, b, NT, preferred_element_type=jnp.float32)


def partner(me, n, i):
    blocks = n // NEAR
    block, place = lax.div(me, NEAR), lax.rem(me, NEAR)
    if i >= n - NEAR:
        return block * NEAR + lax.rem(place + 1 + i - (n - NEAR), NEAR)
    step = i // NEAR
    up = blocks - 1 - step
    up = jnp.where(up <= block, up - 1, up)
    down = jnp.where(step >= block, step + 1, step)
    return jnp.where(2 * block < blocks, up, down) * NEAR + lax.rem(place + i, NEAR)


def kernel(
    n,
    x_hbm,
    g_hbm,
    pi_hbm,
    po_hbm,
    ids_hbm,
    out_ref,
    x_buf,
    g_buf,
    pi_buf,
    po_buf,
    ids_ref,
    x_sum,
    g_sum,
    feat,
    recv,
    gram,
    parts,
    load_sem,
    ids_sem,
    send_a,
    recv_a,
    send_b,
    recv_b,
):
    me = lax.axis_index("row")
    quarter, mine = me // SLICES, me % SLICES
    chunks = x_buf.shape[1] // CHUNK

    ids_copy = pltpu.make_async_copy(ids_hbm, ids_ref, ids_sem)
    ids_copy.start()
    pairs = ((po_hbm, po_buf), (g_hbm, g_buf), (pi_hbm, pi_buf), (x_hbm, x_buf))

    def loads(c):
        cols = pl.ds(pl.multiple_of(c * CHUNK, CHUNK), CHUNK)
        return cols, [
            pltpu.make_async_copy(src.at[:, cols], dst.at[:, cols], load_sem.at[c, i])
            for i, (src, dst) in enumerate(pairs)
        ]

    for i, copy in enumerate(loads(0)[1]):
        copy.start(priority=i // 2)

    barrier = pltpu.get_barrier_semaphore()
    for i in range(n - 1):
        pl.semaphore_signal(
            barrier, inc=1, device_id={"row": partner(me, n, i)}, device_id_type=MESH
        )

    @pl.loop(1, chunks)
    def _(c):
        for i, copy in enumerate(loads(c)[1]):
            copy.start(priority=i // 2)

    g_sum[...] = jnp.zeros_like(g_sum)
    x_sum[...] = jnp.zeros_like(x_sum)

    @pl.loop(0, chunks)
    def _(c):
        cols, copies = loads(c)
        for copy in copies:
            copy.wait()
        g = dot_nt(po_buf[:, cols], g_buf[:, cols])
        x = dot_nt(x_buf[:, cols], pi_buf[:, cols])
        g_sum[...] += g
        x_sum[...] += x

    tokens = x_buf.shape[0]
    g = g_sum[...].astype(jnp.bfloat16).astype(jnp.float32)
    ids_copy.wait()
    ids = ids_ref[...].reshape(1, tokens)
    onehot = (ids == lax.broadcasted_iota(jnp.int32, (EX_DEV, tokens), 0)).astype(jnp.float32)
    masked = (g[:, None, :] * onehot[None, :, :]).reshape(RANK * EX_DEV, tokens)
    weighted = masked.astype(jnp.bfloat16)

    x = x_sum[...]
    x = jnp.concatenate([x, x], axis=1).astype(jnp.bfloat16)
    outer = jnp.dot(weighted, x, preferred_element_type=jnp.float32)
    half = RANK * EX_DEV // 2
    low = lax.broadcasted_iota(jnp.int32, (half, LANES), 1) < RANK
    packed = jnp.where(low, outer[:half], outer[half:]) * (1.0 / math.sqrt(TPE))
    feat[...] = packed.astype(jnp.bfloat16).reshape(feat.shape)

    pl.semaphore_wait(barrier, n - 1)
    for i in range(n - 1):
        target = partner(me, n, i)
        pltpu.make_async_remote_copy(
            src_ref=feat.at[lax.rem(target, SLICES)],
            dst_ref=recv.at[me],
            send_sem=send_a,
            recv_sem=recv_a,
            device_id={"row": target},
            device_id_type=MESH,
        ).start()
    recv[me] = feat[mine]
    rest = recv.at[pl.ds(0, n - 1)]
    pltpu.make_async_copy(rest, rest, recv_a).wait()

    def rows(block):
        block = block.astype(jnp.float32).reshape(-1, 2, EX_DEV, LANES)
        sides = [block[:, i].reshape(-1, LANES) for i in range(2)]
        return jnp.concatenate(sides, axis=1).astype(jnp.bfloat16)

    every = rows(recv[...])
    own = every if n == SLICES else rows(recv[pl.ds(quarter * SLICES, SLICES)])
    gram[...] = dot_nt(own, every).reshape(gram.shape)

    for i in range(SLICES - 1):
        to = partner(mine, SLICES, i)
        pltpu.make_async_remote_copy(
            src_ref=gram.at[to],
            dst_ref=parts.at[mine],
            send_sem=send_b,
            recv_sem=recv_b,
            device_id={"row": quarter * SLICES + to},
            device_id_type=MESH,
        ).start()
    parts[mine] = gram[mine]
    rest_b = parts.at[pl.ds(0, SLICES - 1)]
    pltpu.make_async_copy(rest_b, rest_b, recv_b).wait()
    out_ref[...] = jnp.sum(parts[...], axis=0) * (1.0 / RANK)
    pltpu.make_async_copy(rest, rest, send_a).wait()
    pltpu.make_async_copy(rest_b, rest_b, send_b).wait()


def shards(n, inputs, out_grads, proj_in, proj_out, example_ids):
    tokens, width = inputs.shape
    examples = EX_DEV * n
    hbm = pl.BlockSpec(memory_space=pl.ANY)
    vmem = pl.BlockSpec(memory_space=pltpu.VMEM)
    flops = 4 * tokens * width * RANK
    return pl.pallas_call(
        functools.partial(kernel, n),
        out_shape=pltpu.VMEM((EX_DEV, examples), jnp.float32),
        in_specs=[hbm] * 5,
        out_specs=vmem,
        scratch_shapes=[
            pltpu.VMEM((tokens, width), jnp.bfloat16),
            pltpu.VMEM((tokens, width), jnp.bfloat16),
            pltpu.VMEM((RANK, width), jnp.bfloat16),
            pltpu.VMEM((RANK, width), jnp.bfloat16),
            pltpu.VMEM((tokens,), jnp.int32),
            pltpu.VMEM((tokens, RANK), jnp.float32),
            pltpu.VMEM((RANK, tokens), jnp.float32),
            pltpu.VMEM((SLICES, 2 * EX_DEV, LANES), jnp.bfloat16),
            pltpu.VMEM((n, 2 * EX_DEV, LANES), jnp.bfloat16),
            pltpu.VMEM((SLICES, EX_DEV, examples), jnp.float32),
            pltpu.VMEM((SLICES, EX_DEV, examples), jnp.float32),
            pltpu.SemaphoreType.DMA((width // CHUNK, 4)),
            pltpu.SemaphoreType.DMA,
            pltpu.SemaphoreType.DMA,
            pltpu.SemaphoreType.DMA,
            pltpu.SemaphoreType.DMA,
            pltpu.SemaphoreType.DMA,
        ],
        compiler_params=pltpu.CompilerParams(
            collective_id=0, has_side_effects=True, vmem_limit_bytes=63 * 1024 * 1024
        ),
        cost_estimate=pl.CostEstimate(
            flops=flops, bytes_accessed=4 * (tokens + RANK) * width, transcendentals=0
        ),
    )(inputs, out_grads, proj_in.T, proj_out.T, example_ids)


def solution(mesh):
    in_specs = (P(("grp", "row"), None), P(("grp", "row"), None), P(), P(), P(("grp", "row")))
    out_specs = P(("grp", "row"), None)
    body = functools.partial(shards, mesh.shape["row"])
    return jax.shard_map(body, mesh=mesh, in_specs=in_specs, out_specs=out_specs, check_vma=False)
```
